256 devices in a mesh: rep: 8 (over y, core), fsdp: 32 (over z, x).
Axes of the slice: x: 4, y: 4, z: 8, core: 2. Of those that a mesh axis runs over, the one named last changes fastest.
Arguments:
- momentum: float32 [8, 3072, 12288], P('rep', 'fsdp')
- kept: int32 [3072, 192, 4], P('fsdp'), may hold values from 0 to 63, as said below
- counts: int32 [8, 3072, 192], P(None, 'fsdp'), may hold values from 1 to 4, 384 in all within a row
Outputs:
- new_momentum: float32 [8, 3072, 12288], P('rep', 'fsdp')
- update: bfloat16 [3072, 12288], P('fsdp')
The draws below stay inside these ranges and needn't reach their ends.
Inputs may be any that keep to these rules, and one draw needn't show every extreme that they name: `kept`: the 4 numbers listed for one block are distinct. The counts of one row of one replica sum to 384.
All inputs are finite; a program needn't handle non-finite values.
Results may differ from the reference program's by a relative error of at most 0.001.
Values sent between devices are 32-bit elements; how exact they have to be, the bound alone decides.
No kernel may reach another device: no remote copies, remote signals or barrier semaphores. Data moves between devices by JAX's collectives and lax.ppermute only.
A program may use at most 256 MiB of HBM per device.

```python
import math
import jax
import jax.numpy as jnp
import numpy as np
from jax import lax

D = 3072
FF = 12288
CH = 64
KEEP = 4
ROW_KEPT = 384
N_REP = 8


def draw_momentum(key, part):
    key = jax.random.fold_in(key, 5)
    key_noise, key_column = jax.random.split(key, 2)
    row_level = lax.broadcasted_iota(jnp.float32, (1, D, 1), 1) / D
    row_scale = jnp.exp(row_level * math.log(10.0))
    column_scale = jnp.exp(jax.random.uniform(key_column, (1, 1, FF), jnp.float32) * math.log(10.0))
    noise = jnp.clip(jax.random.normal(key_noise, (N_REP, D, FF), jnp.float32), -6.0, 6.0)
    return 0.2 * noise * row_scale * column_scale


def draw_kept(key, part):
    key = jax.random.fold_in(key, 11)
    key_step, key_flip = jax.random.split(key)
    block_shape = (D, FF // CH, 1)
    stride = 2 * jax.random.randint(key_step, block_shape, 0, CH // 2) + 1
    flips = jax.random.randint(key_flip, block_shape, 0, CH)
    slot_ids = lax.broadcasted_iota(jnp.int32, (D, FF // CH, KEEP), 2)
    return jnp.bitwise_xor(slot_ids * stride % CH, flips).astype(jnp.int32)


def profile(count, total, reach, slope):
    weights = [(1 << 20) // math.isqrt(standing ** slope) + 1 for standing in range(2, count + 1)]
    surplus, holding = total - reach - (count - 1), [1] * (count - 1)
    while surplus > 0:
        movable = [i for i in range(count - 1) if holding[i] < reach]
        pool, left = sum([weights[i] for i in movable]), surplus
        for i in movable:
            extra = min(reach - holding[i], max(1, left * weights[i] // pool), surplus)
            holding[i] = holding[i] + extra
            surplus = surplus - extra
    return np.array([reach] + holding)


def uneven(key, count, total, most, lean):
    if count == 2:
        one = jax.random.randint(key, (), max(1, total - most), min(most, total - 1) + 1)
        return jnp.stack([one, total - one])
    lengths = jnp.asarray(profile(count, total, most, lean), jnp.int32)
    couples = (count - 1) // 2
    giver, sink = lengths[1:1 + 2 * couples:2], lengths[2:2 + 2 * couples:2]
    margin = jnp.minimum(giver - 1, most - sink)
    passed = jax.random.randint(jax.random.fold_in(key, 1), (couples,), 0, 1 << 20) % (margin + 1)
    lengths = lengths.at[1:1 + 2 * couples:2].set(giver - passed).at[2:2 + 2 * couples:2].set(sink + passed)
    return lengths[jax.random.permutation(jax.random.fold_in(key, 2), count)]


def setup_inputs(seed: int = 0) -> dict:
    key_of = jax.random.split(jax.random.key(seed), 4)
    return {
        "momentum": draw_momentum(jax.random.fold_in(key_of[3], 71), 0),
        "kept": draw_kept(jax.random.fold_in(key_of[3], 71), 0),
        "counts": jax.vmap(lambda own: uneven(own, FF // CH, ROW_KEPT, KEEP, 2))(jax.random.split(key_of[2], N_REP * D)).reshape((N_REP, D, FF // CH)).astype(jnp.int32),
    }


def dct_table(length):
    frequency = lax.broadcasted_iota(jnp.float32, (length, length), 0)
    position = lax.broadcasted_iota(jnp.float32, (length, length), 1)
    waves = jnp.cos(math.pi * (2.0 * position + 1.0) * frequency / (2.0 * length))
    scaling = jnp.where(frequency == 0, math.sqrt(1.0 / length), math.sqrt(2.0 / length))
    return waves * scaling

def reference(momentum, kept, counts):
    basis_table = dct_table(CH)
    nchunk = FF // CH
    slot_shape = (D, nchunk, KEEP)
    slot_ids = lax.broadcasted_iota(jnp.int32, slot_shape, 2)
    group_ids = lax.broadcasted_iota(jnp.int32, slot_shape, 1)
    row_ids = lax.broadcasted_iota(jnp.int32, slot_shape, 0)
    places = (row_ids * FF + group_ids * CH + kept).reshape(-1).astype(jnp.int32)

    def replica_step(running, inputs):
        moment, count_row = inputs
        coeffs = jnp.dot(moment.reshape(-1, CH), basis_table.T, precision=lax.Precision.HIGHEST).reshape(D, nchunk, CH)
        picked = jnp.take_along_axis(coeffs, kept, axis=2)
        picked = jnp.where(slot_ids < count_row[..., None], picked, 0.0)
        sent_dense = jnp.zeros((D * FF,), jnp.float32).at[places].add(picked.reshape(-1))
        decoded = jnp.dot(sent_dense.reshape(-1, CH), basis_table, precision=lax.Precision.HIGHEST).reshape(D, FF)
        return (running + sent_dense, moment - decoded)
    summed_dense, new_momentum = lax.scan(replica_step, jnp.zeros((D * FF,), jnp.float32), (momentum, counts))
    raw = jnp.dot(summed_dense.reshape(-1, CH), basis_table, precision=lax.Precision.HIGHEST).reshape(D, FF) / N_REP
    energy = jnp.sum(raw * raw)
    update = (raw * lax.rsqrt(energy / (D * FF) + 1e-06)).astype(jnp.bfloat16)
    return (new_momentum, update)
```

```python
import functools
import math

import jax
import jax.numpy as jnp
import ml_dtypes
import numpy as np
from jax import lax
from jax.experimental import pallas as pl
from jax.experimental.pallas import tpu as pltpu
from jax.sharding import PartitionSpec as P

CH = 64
KEEP = 4
LANES = 128
PAIR = LANES // CH
CELLS = LANES // KEEP
TILES = CELLS // PAIR
WIDTH = TILES * LANES


def pair_table():
    k, n = np.arange(CH)[:, None], np.arange(CH)[None, :]
    basis = np.cos(math.pi * (2 * n + 1) * k / (2 * CH)) * math.sqrt(2 / CH)
    basis[0] = math.sqrt(1 / CH)
    return np.kron(np.eye(PAIR), basis)


def split_weights(table):
    high = table.astype(ml_dtypes.bfloat16)
    low = (table - high.astype(np.float64)).astype(ml_dtypes.bfloat16)
    side = np.concatenate([high, low], axis=1)
    return np.concatenate([side, side], axis=0)


def halves(x):
    high = x.astype(jnp.bfloat16)
    low = (x - high.astype(jnp.float32)).astype(jnp.bfloat16)
    return jnp.concatenate([high, low], axis=1)


def apply_table(tiles, weights):
    rows = tiles[0].shape[0]
    stacked = jnp.concatenate([halves(tile) for tile in tiles], axis=0)
    out = jnp.dot(stacked, weights, preferred_element_type=jnp.float32)
    out = out[:, :LANES] + out[:, LANES:]
    return [out[i * rows : (i + 1) * rows] for i in range(len(tiles))]


def lane_gather(x, index):
    return jnp.take_along_axis(x, index, axis=1, mode="promise_in_bounds")


def lane_ids(rows):
    return lax.broadcasted_iota(jnp.int32, (rows, LANES), 1)


def spread(ref_value, group, rows):
    start = group * CELLS
    base = start // LANES * LANES
    part = ref_value[:, base : base + LANES]
    if part.shape[1] < LANES:
        part = jnp.pad(part, ((0, 0), (0, LANES - part.shape[1])))
    return lane_gather(part, start - base + lane_ids(rows) % CELLS)


def pick_kernel(groups, rep_ref, x_ref, kept_ref, cnt_ref, w_ref, slot_ref, mine_ref, other_ref, scr):
    step = pl.program_id(0)
    rows = x_ref.shape[1]
    lanes = lane_ids(rows)
    slot = lanes // CELLS
    cell = lanes % CELLS

    @pl.when(step == 0)
    def _():
        counts = cnt_ref[0]
        numbers = [kept_ref[:, s, :] for s in range(KEEP)]
        for g in range(groups):
            chosen = spread(numbers[0], g, rows)
            for s in range(1, KEEP):
                chosen = jnp.where(slot == s, spread(numbers[s], g, rows), chosen)
            live = slot < spread(counts, g, rows)
            slot_ref[g] = chosen
            scr[g] = jnp.where(live, 1.0, 0.0)

    index = slot_ref[step] + (cell % PAIR) * CH
    picked = jnp.zeros((rows, LANES), jnp.float32)
    batch = 8
    for first in range(0, TILES, batch):
        tiles = [x_ref[0, :, t * LANES : (t + 1) * LANES] for t in range(first, first + batch)]
        for t, coeffs in enumerate(apply_table(tiles, w_ref[...]), first):
            picked = jnp.where(cell // PAIR == t, lane_gather(coeffs, index), picked)
    picked = jnp.where(scr[step] > 0.0, picked, 0.0)
    half = groups // 2
    core = rep_ref[0] % 2
    here = step // half == core

    @pl.when(here)
    def _():
        mine_ref[step % half] = picked

    @pl.when(jnp.logical_not(here))
    def _():
        other_ref[step % half] = picked


def group_values(rep_ref, mine_ref, other_ref, step, half):
    here = step // half == rep_ref[0] % 2
    place = step % half
    return jnp.where(here, mine_ref[place], other_ref[place])


def residue_kernel(groups, rep_ref, x_ref, slot_ref, mine_ref, other_ref, w_ref, out_ref, place_ref):
    step = pl.program_id(0)
    rows = x_ref.shape[1]
    lanes = lane_ids(rows)
    values = group_values(rep_ref, mine_ref, other_ref, step, groups // 2)
    numbers = slot_ref[step]
    batch = 8
    for first in range(0, TILES, batch):
        dense = []
        for t in range(first, first + batch):
            place = jnp.full((rows, LANES), -1, jnp.int32)
            for s in range(KEEP):
                source = s * CELLS + t * PAIR + lanes // CH
                place = jnp.where(lane_gather(numbers, source) == lanes % CH, source, place)
            place_ref[step, t] = place
            dense.append(jnp.where(place >= 0, lane_gather(values, place & (LANES - 1)), 0.0))
        for t, decoded in enumerate(apply_table(dense, w_ref[...]), first):
            part = slice(t * LANES, (t + 1) * LANES)
            out_ref[0, :, part] = x_ref[0, :, part] - decoded


def update_kernel(groups, entries, replicas, rep_ref, place_ref, mine_ref, other_ref, energy_ref, w_ref, out_ref):
    step = pl.program_id(0)
    energy = jnp.sum(energy_ref[:, 0, :], axis=0, keepdims=True)
    scale = lax.rsqrt(energy / entries + 1e-06) / replicas
    values = group_values(rep_ref, mine_ref, other_ref, step, groups // 2) * scale
    batch = 8
    for first in range(0, TILES, batch):
        dense = []
        for t in range(first, first + batch):
            place = place_ref[step, t]
            dense.append(jnp.where(place >= 0, lane_gather(values, place & (LANES - 1)), 0.0))
        for t, decoded in enumerate(apply_table(dense, w_ref[...]), first):
            out_ref[:, t * LANES : (t + 1) * LANES] = decoded.astype(jnp.bfloat16)


def per_device(momentum, kept, counts):
    _, rows, width = momentum.shape
    blocks = width // CH
    groups = width // WIDTH
    half = groups // 2
    replicas = lax.axis_size("rep")
    shards = lax.axis_size("fsdp")
    rep = lax.axis_index("rep").astype(jnp.int32).reshape(1)
    basis = pair_table()
    forward = jnp.asarray(split_weights(basis.T))
    inverse = jnp.asarray(split_weights(basis))
    slots = jnp.transpose(kept, (0, 2, 1))

    def whole(shape):
        return pl.BlockSpec(shape, lambda g, rep_ref: (0,) * len(shape))

    half_shape = (half, rows, LANES)
    half_out = jax.ShapeDtypeStruct(half_shape, jnp.float32)
    x_spec = pl.BlockSpec((1, rows, WIDTH), lambda g, rep_ref: (0, 0, g))
    w_spec = whole(forward.shape)
    numbers, mine, other = pl.pallas_call(
        functools.partial(pick_kernel, groups),
        grid_spec=pltpu.PrefetchScalarGridSpec(
            num_scalar_prefetch=1,
            grid=(groups,),
            in_specs=[
                x_spec,
                whole((rows, KEEP, blocks)),
                pl.BlockSpec((1, rows, blocks), lambda g, rep_ref: (rep_ref[0], 0, 0)),
                w_spec,
            ],
            out_specs=[whole((groups, rows, LANES)), whole(half_shape), whole(half_shape)],
            scratch_shapes=[pltpu.VMEM((groups, rows, LANES), jnp.float32)],
        ),
        out_shape=[jax.ShapeDtypeStruct((groups, rows, LANES), jnp.int32), half_out, half_out],
        compiler_params=pltpu.CompilerParams(vmem_limit_bytes=32 << 20),
        name="pick",
    )(rep, momentum, slots, counts, forward)

    swap = [(i, i ^ 1) for i in range(replicas)]
    flat = (half * rows, LANES)
    chip = mine.reshape(flat) + lax.ppermute(other.reshape(flat), "rep", swap)
    parts = [chip]
    for away in (4, 2, 6):
        ring = [(i, (i + away) % replicas) for i in range(replicas)]
        parts.append(lax.ppermute(chip, "rep", ring))
    total = (parts[0] + parts[1]) + (parts[2] + parts[3])
    total_other = lax.ppermute(total, "rep", swap)

    new_moment, place = pl.pallas_call(
        functools.partial(residue_kernel, groups),
        grid_spec=pltpu.PrefetchScalarGridSpec(
            num_scalar_prefetch=1,
            grid=(groups,),
            in_specs=[
                x_spec,
                whole((groups, rows, LANES)),
                whole(half_shape),
                whole(half_shape),
                w_spec,
            ],
            out_specs=[x_spec, whole((groups, TILES, rows, LANES))],
        ),
        out_shape=[
            jax.ShapeDtypeStruct(momentum.shape, jnp.float32),
            jax.ShapeDtypeStruct((groups, TILES, rows, LANES), jnp.int32),
        ],
        compiler_params=pltpu.CompilerParams(vmem_limit_bytes=32 << 20),
        name="residue",
    )(rep, momentum, numbers, mine, other, inverse)

    energy = jnp.sum(jnp.square(total / replicas)) + jnp.sum(jnp.square(total_other / replicas))
    energies = lax.all_to_all(
        jnp.full((shards, 1, LANES), energy, jnp.float32), "fsdp", 0, 0, tiled=True
    )
    update = pl.pallas_call(
        functools.partial(update_kernel, groups, rows * width * shards, replicas),
        grid_spec=pltpu.PrefetchScalarGridSpec(
            num_scalar_prefetch=1,
            grid=(groups,),
            in_specs=[
                whole((groups, TILES, rows, LANES)),
                whole(half_shape),
                whole(half_shape),
                whole((shards, 1, LANES)),
                w_spec,
            ],
            out_specs=pl.BlockSpec((rows, WIDTH), lambda g, rep_ref: (0, g)),
        ),
        out_shape=jax.ShapeDtypeStruct((rows, width), jnp.bfloat16),
        compiler_params=pltpu.CompilerParams(vmem_limit_bytes=32 << 20),
        name="update",
    )(rep, place, total.reshape(half_shape), total_other.reshape(half_shape), energies, inverse)
    return new_moment, update


def solution(mesh):
    placed = (P("rep", "fsdp", None), P("fsdp", None, None), P(None, "fsdp", None))
    return jax.shard_map(
        per_device,
        mesh=mesh,
        in_specs=placed,
        out_specs=(P("rep", "fsdp", None), P("fsdp", None)),
        check_vma=False,
    )
```

```python
import functools
import math

import jax
import jax.numpy as jnp
import ml_dtypes
import numpy as np
from jax import lax
from jax.experimental import pallas as pl
from jax.experimental.pallas import tpu as pltpu
from jax.sharding import PartitionSpec as P

CH = 64
KEEP = 4
LANES = 128
PACK = 16
PAIR = LANES // CH
CELLS = LANES // KEEP
TILES = CELLS // PAIR
WIDTH = TILES * LANES
BF = jnp.bfloat16
VMEM_BYTES = 32 << 20


def pair_table():
    k, n = np.arange(CH)[:, None], np.arange(CH)[None, :]
    basis = np.cos(math.pi * (2 * n + 1) * k / (2 * CH)) * math.sqrt(2 / CH)
    basis[0] = math.sqrt(1 / CH)
    return np.kron(np.eye(PAIR), basis)


def split_weights(table):
    high = table.astype(ml_dtypes.bfloat16)
    low = (table - high.astype(np.float64)).astype(ml_dtypes.bfloat16)
    side = np.concatenate([high, low], axis=1)
    return np.concatenate([side, side], axis=0)


def halves(x):
    high = x.astype(BF)
    return high, (x - high.astype(jnp.float32)).astype(BF)


def apply_weights(tiles, weights):
    rows = tiles[0].shape[0]
    out = jnp.dot(jnp.concatenate(tiles, axis=0), weights, preferred_element_type=jnp.float32)
    out = out[:, :LANES] + out[:, LANES:]
    return [out[i * rows : (i + 1) * rows] for i in range(len(tiles))]


def lane_gather(x, index):
    return jnp.take_along_axis(x, index, axis=1, mode="promise_in_bounds")


def lane_ids(rows):
    return lax.broadcasted_iota(jnp.int32, (rows, LANES), 1)


def spread(value, group, rows):
    start = group * CELLS
    base = start // LANES * LANES
    part = value[:, base : base + LANES]
    if part.shape[1] < LANES:
        part = jnp.pad(part, ((0, 0), (0, LANES - part.shape[1])))
    return lane_gather(part, start - base + lane_ids(rows) % CELLS)


def flip(x):
    fill = LANES - x.shape[0]
    return jnp.concatenate([x, x[:fill]], axis=0).T if fill else x.T


def columns(group):
    return pl.ds(pl.multiple_of(group * WIDTH, WIDTH), WIDTH)


def pick_kernel(
    rep_ref, x_hbm, kept_hbm, cnt_hbm, w_hbm, flip_ref, mine_ref, other_ref, x_ref,
    kept_ref, cnt_ref, w_ref, index_ref, live_ref, coeff_ref, small_sem, x_sem,
):
    groups, rows, _ = x_ref.shape
    half = groups // 2
    small = [
        pltpu.make_async_copy(kept_hbm, kept_ref, small_sem.at[0]),
        pltpu.make_async_copy(cnt_hbm.at[rep_ref[0]], cnt_ref, small_sem.at[1]),
        pltpu.make_async_copy(w_hbm, w_ref, small_sem.at[2]),
    ]
    for copy in small:
        copy.start()
    for g in range(groups):
        pltpu.make_async_copy(x_hbm.at[0, :, columns(g)], x_ref.at[g], x_sem.at[g]).start()
    for copy in small:
        copy.wait()

    lanes = lane_ids(rows)
    slot = lanes // CELLS
    counts = cnt_ref[...]
    numbers = [kept_ref[:, s, :] for s in range(KEEP)]
    for g in range(groups):
        chosen = spread(numbers[0], g, rows)
        for s in range(1, KEEP):
            chosen = jnp.where(slot == s, spread(numbers[s], g, rows), chosen)
        index_ref[g] = chosen + lanes % PAIR * CH
        flip_ref[g] = flip(chosen.astype(jnp.float32))
        live_ref[g] = jnp.where(slot < spread(counts, g, rows), 1.0, 0.0)

    tile_of = lane_ids(8) % CELLS // PAIR
    core = rep_ref[0] % 2

    def body(g, carry):
        pltpu.make_async_copy(x_hbm.at[0, :, columns(g)], x_ref.at[g], x_sem.at[g]).wait()
        tiles = [
            jnp.concatenate(halves(x_ref[g, :, t * LANES : (t + 1) * LANES]), axis=1)
            for t in range(TILES)
        ]
        for t, coeffs in enumerate(apply_weights(tiles, w_ref[...])):
            coeff_ref[t] = coeffs
        parts = []
        for first in range(0, rows, 8):
            here = slice(first, first + 8)
            index = index_ref[g, here]
            picked = jnp.zeros((8, LANES), jnp.float32)
            for t in range(TILES):
                picked = jnp.where(tile_of == t, lane_gather(coeff_ref[t, here], index), picked)
            parts.append(jnp.where(live_ref[g, here] > 0.0, picked, 0.0))
        picked = jnp.concatenate(parts, axis=0)

        @pl.when(g // half == core)
        def _():
            mine_ref[g % half] = picked

        @pl.when(g // half != core)
        def _():
            other_ref[g % half] = picked

        return carry

    lax.fori_loop(0, groups, body, 0)


def decode_group(flip_ref, g, values, w_ref, high_ref, low_ref):
    rows = values.shape[0]
    turned = flip(values)
    high = turned.astype(BF).astype(jnp.float32)
    high_ref[...] = high
    low_ref[...] = turned - high
    number = lax.broadcasted_iota(jnp.int32, (PACK, LANES), 0).astype(jnp.float32)
    zero = jnp.zeros((PACK, LANES), BF)

    def row(values_ref, s, cell):
        at = s * CELLS + cell
        return jnp.broadcast_to(values_ref[at : at + 1, :], (PACK, LANES)).astype(BF)

    tiles = []
    for t in range(TILES):
        highs, lows = [], []
        for cell in range(t * PAIR, (t + 1) * PAIR):
            kept = [row(flip_ref.at[g], s, cell) for s in range(KEEP)]
            cell_high = [row(high_ref, s, cell) for s in range(KEEP)]
            cell_low = [row(low_ref, s, cell) for s in range(KEEP)]
            for first in range(0, CH, PACK):
                ids = (number + first).astype(BF)
                dense_high, dense_low = zero, zero
                for s in range(KEEP):
                    hit = kept[s] == ids
                    dense_high = jnp.where(hit, cell_high[s], dense_high)
                    dense_low = jnp.where(hit, cell_low[s], dense_low)
                highs.append(dense_high)
                lows.append(dense_low)
        both = [jnp.concatenate(part, axis=0).T[:rows] for part in (highs, lows)]
        tiles.append(jnp.concatenate(both, axis=1))
    return apply_weights(tiles, w_ref[...])


def side(rep_ref, mine_ref, other_ref, g):
    half = mine_ref.shape[0]
    return jnp.where(g // half == rep_ref[0] % 2, mine_ref[g % half], other_ref[g % half])


def residue_kernel(
    rep_ref, x_ref, flip_ref, mine_ref, other_ref, w_ref, after_ref, out_hbm, done_ref,
    high_ref, low_ref, out_ref, sem,
):
    groups = x_ref.shape[0]
    done_ref[...] = jnp.zeros(done_ref.shape, jnp.float32)

    def copy(g):
        return pltpu.make_async_copy(out_ref.at[g], out_hbm.at[0, :, columns(g)], sem.at[g])

    def body(g, carry):
        values = side(rep_ref, mine_ref, other_ref, g)
        for t, part in enumerate(decode_group(flip_ref, g, values, w_ref, high_ref, low_ref)):
            here = slice(t * LANES, (t + 1) * LANES)
            out_ref[g, :, here] = x_ref[g, :, here] - part
        copy(g).start()
        return carry

    lax.fori_loop(0, groups, body, 0)
    for g in range(groups):
        copy(g).wait()


def total_kernel(a_ref, b_ref, c_ref, d_ref, after_ref, out_ref):
    out_ref[...] = (a_ref[...] + b_ref[...]) + (c_ref[...] + d_ref[...])


def energy_kernel(replicas, a_ref, b_ref, out_ref):
    square = jnp.square(a_ref[...] / replicas) + jnp.square(b_ref[...] / replicas)
    energy = jnp.sum(jnp.sum(square, axis=0, keepdims=True), axis=1, keepdims=True)
    out_ref[...] = jnp.broadcast_to(energy[None], out_ref.shape)


def update_kernel(
    entries, replicas, rep_ref, flip_ref, mine_ref, other_ref, energy_ref, w_ref, out_hbm,
    high_ref, low_ref, out_ref, sem,
):
    groups = out_ref.shape[0]
    energy = jnp.sum(energy_ref[:, 0, :], axis=0, keepdims=True)
    scale = lax.rsqrt(energy / entries + 1e-06) / replicas

    def copy(g):
        return pltpu.make_async_copy(out_ref.at[g], out_hbm.at[:, columns(g)], sem.at[g])

    def body(g, carry):
        values = side(rep_ref, mine_ref, other_ref, g) * scale
        for t, part in enumerate(decode_group(flip_ref, g, values, w_ref, high_ref, low_ref)):
            out_ref[g, :, t * LANES : (t + 1) * LANES] = part.astype(BF)
        copy(g).start()
        return carry

    lax.fori_loop(0, groups, body, 0)
    for g in range(groups):
        copy(g).wait()


def call(kernel, name, operands, out_shape, scratch=(), microseconds=1.0):
    specs, arrays = [], []
    for place, array in operands:
        specs.append(pl.BlockSpec(memory_space=place))
        arrays.append(pltpu.with_memory_space_constraint(array, place) if place is pltpu.HBM else array)
    shapes = out_shape if isinstance(out_shape, list) else [out_shape]
    outs = [
        pl.BlockSpec(memory_space=pltpu.HBM if shape.memory_space is pltpu.HBM else pltpu.VMEM)
        for shape in shapes
    ]
    return pl.pallas_call(
        kernel,
        in_specs=specs,
        out_specs=outs if isinstance(out_shape, list) else outs[0],
        out_shape=out_shape,
        scratch_shapes=list(scratch),
        compiler_params=pltpu.CompilerParams(vmem_limit_bytes=VMEM_BYTES),
        cost_estimate=pl.CostEstimate(
            flops=0, bytes_accessed=int(microseconds * 3.0e6), transcendentals=0
        ),
        name=name,
    )(*arrays)


def per_device(momentum, kept, counts):
    _, rows, width = momentum.shape
    blocks = width // CH
    groups = width // WIDTH
    half = groups // 2
    replicas = lax.axis_size("rep")
    shards = lax.axis_size("fsdp")
    rep = lax.axis_index("rep").astype(jnp.int32).reshape(1)
    basis = pair_table()
    forward = jnp.asarray(split_weights(basis.T))
    inverse = jnp.asarray(split_weights(basis))
    hbm, vmem, smem = pltpu.HBM, pltpu.VMEM, pltpu.SMEM
    half_shape = (half, rows, LANES)
    flat = (half * rows, LANES)
    dma = pltpu.SemaphoreType.DMA
    turned = [vmem((LANES, LANES), jnp.float32)] * 2

    flipped, mine, other, x = call(
        pick_kernel,
        "pick",
        [
            (smem, rep),
            (hbm, momentum),
            (hbm, jnp.transpose(kept, (0, 2, 1))),
            (hbm, counts),
            (hbm, forward),
        ],
        [
            vmem((groups, LANES, LANES), jnp.float32),
            vmem(half_shape, jnp.float32),
            vmem(half_shape, jnp.float32),
            vmem((groups, rows, WIDTH), jnp.float32),
        ],
        [
            vmem((rows, KEEP, blocks), jnp.int32),
            vmem((rows, blocks), jnp.int32),
            vmem(forward.shape, BF),
            vmem((groups, rows, LANES), jnp.int32),
            vmem((groups, rows, LANES), jnp.float32),
            vmem((TILES, rows, LANES), jnp.float32),
            dma((3,)),
            dma((groups,)),
        ],
        5.0,
    )

    swap = [(i, i ^ 1) for i in range(replicas)]
    chip = mine.reshape(flat) + lax.ppermute(other.reshape(flat), "rep", swap)
    away = []
    for step in (4, 2, 6):
        ring = [(i, (i + step) % replicas) for i in range(replicas)]
        away.append(lax.ppermute(chip, "rep", ring))

    new_moment, done = call(
        residue_kernel,
        "residue",
        [(smem, rep), (vmem, x), (vmem, flipped), (vmem, mine), (vmem, other), (vmem, inverse), (vmem, chip)],
        [hbm(momentum.shape, jnp.float32), vmem((8, LANES), jnp.float32)],
        turned + [vmem((groups, rows, WIDTH), jnp.float32), dma((groups,))],
        5.0,
    )
    total = call(
        total_kernel,
        "total",
        [(vmem, chip)] + [(vmem, part) for part in away] + [(vmem, done)],
        vmem(flat, jnp.float32),
        microseconds=0.5,
    )
    total_other = lax.ppermute(total, "rep", swap)
    energies = call(
        functools.partial(energy_kernel, replicas),
        "energy",
        [(vmem, total), (vmem, total_other)],
        vmem((shards, 1, LANES), jnp.float32),
        microseconds=0.5,
    )
    energies = lax.all_to_all(energies, "fsdp", 0, 0, tiled=True)
    update = call(
        functools.partial(update_kernel, rows * width * shards, replicas),
        "update",
        [
            (smem, rep),
            (vmem, flipped),
            (vmem, total.reshape(half_shape)),
            (vmem, total_other.reshape(half_shape)),
            (vmem, energies),
            (vmem, inverse),
        ],
        hbm((rows, width), BF),
        turned + [vmem((groups, rows, WIDTH), BF), dma((groups,))],
        4.0,
    )
    return new_moment, update


def solution(mesh):
    placed = (P("rep", "fsdp", None), P("fsdp", None, None), P(None, "fsdp", None))
    return jax.shard_map(
        per_device,
        mesh=mesh,
        in_specs=placed,
        out_specs=(P("rep", "fsdp", None), P("fsdp", None)),
        check_vma=False,
    )
```

```python
import functools
import math

import jax
import jax.numpy as jnp
import ml_dtypes
import numpy as np
from jax import lax
from jax.experimental import pallas as pl
from jax.experimental.pallas import tpu as pltpu
from jax.sharding import PartitionSpec as P

CH = 64
KEEP = 4
LANES = 128
PACK = 16
PAIR = LANES // CH
CELLS = LANES // KEEP
TILES = CELLS // PAIR
WIDTH = TILES * LANES
BF = jnp.bfloat16
VMEM_BYTES = 32 << 20
CHUNKS = 4


def pair_table():
    k, n = np.arange(CH)[:, None], np.arange(CH)[None, :]
    basis = np.cos(math.pi * (2 * n + 1) * k / (2 * CH)) * math.sqrt(2 / CH)
    basis[0] = math.sqrt(1 / CH)
    return np.kron(np.eye(PAIR), basis)


def split_weights(table):
    high = table.astype(ml_dtypes.bfloat16)
    low = (table - high.astype(np.float64)).astype(ml_dtypes.bfloat16)
    side = np.concatenate([high, low], axis=1)
    return np.concatenate([side, side], axis=0)


def halves(x):
    high = x.astype(BF)
    return high, (x - high.astype(jnp.float32)).astype(BF)


def apply_weights(tiles, weights):
    rows = tiles[0].shape[0]
    out = jnp.dot(jnp.concatenate(tiles, axis=0), weights, preferred_element_type=jnp.float32)
    out = out[:, :LANES] + out[:, LANES:]
    return [out[i * rows : (i + 1) * rows] for i in range(len(tiles))]


def lane_gather(x, index):
    return jnp.take_along_axis(x, index, axis=1, mode="promise_in_bounds")


def lane_ids(rows):
    return lax.broadcasted_iota(jnp.int32, (rows, LANES), 1)


def spread(value, group, rows):
    start = group * CELLS
    base = start // LANES * LANES
    part = value[:, base : base + LANES]
    if part.shape[1] < LANES:
        part = jnp.pad(part, ((0, 0), (0, LANES - part.shape[1])))
    return lane_gather(part, start - base + lane_ids(rows) % CELLS)


def flip(x):
    fill = LANES - x.shape[0]
    return jnp.concatenate([x, x[:fill]], axis=0).T if fill else x.T


def columns(group):
    return pl.ds(pl.multiple_of(group * WIDTH, WIDTH), WIDTH)


def pick_kernel(
    rep_ref, x_hbm, kept_hbm, cnt_hbm, w_hbm, number_ref, mine_ref, other_ref, x_ref,
    kept_ref, cnt_ref, w_ref, live_ref, coeff_ref, small_sem, x_sem,
):
    groups, rows, _ = x_ref.shape
    half = groups // 2
    small = [
        pltpu.make_async_copy(w_hbm, w_ref, small_sem.at[0]),
        pltpu.make_async_copy(kept_hbm, kept_ref, small_sem.at[1]),
        pltpu.make_async_copy(cnt_hbm.at[rep_ref[0]], cnt_ref, small_sem.at[2]),
    ]
    for copy in small:
        copy.start()

    def x_copy(g):
        return pltpu.make_async_copy(x_hbm.at[0, :, columns(g)], x_ref.at[g], x_sem.at[g])

    for g in range(groups):
        x_copy(g).start()
    for copy in small:
        copy.wait()

    slot = lane_ids(rows) // CELLS
    counts = cnt_ref[...]
    numbers = [kept_ref[:, s, :] for s in range(KEEP)]
    for g in range(groups):
        chosen = spread(numbers[0], g, rows)
        for s in range(1, KEEP):
            chosen = jnp.where(slot == s, spread(numbers[s], g, rows), chosen)
        number_ref[g] = chosen
        live_ref[g] = jnp.where(slot < spread(counts, g, rows), 1.0, 0.0)

    lanes = lane_ids(8)
    block_start = lanes % PAIR * CH
    tile_of = lanes % CELLS // PAIR
    core = rep_ref[0] % 2

    def transform(g, buffer, tiles):
        parts = [
            jnp.concatenate(halves(x_ref[g, :, t * LANES : (t + 1) * LANES]), axis=1) for t in tiles
        ]
        for t, coeffs in zip(tiles, apply_weights(parts, w_ref[...])):
            coeff_ref[buffer, t] = coeffs

    def choose(g, buffer, first):
        here = slice(first, first + 8)
        index = number_ref[g, here] + block_start
        picked = jnp.zeros((8, LANES), jnp.float32)
        for t in range(TILES):
            picked = jnp.where(tile_of == t, lane_gather(coeff_ref[buffer, t, here], index), picked)
        return jnp.where(live_ref[g, here] > 0.0, picked, 0.0)

    def put(g, parts):
        picked = jnp.concatenate(parts, axis=0)

        @pl.when(g // half == core)
        def _():
            mine_ref[g % half] = picked

        @pl.when(g // half != core)
        def _():
            other_ref[g % half] = picked

    def step(g, buffer):
        x_copy(g + 1).wait()
        parts = []
        for j in range(CHUNKS):
            transform(g + 1, 1 - buffer, span(TILES, j))
            parts += [choose(g, buffer, 8 * i) for i in span(rows // 8, j)]
        put(g, parts)

    x_copy(0).wait()
    transform(0, 0, range(TILES))
    two_by_two(step, groups - 1)
    last = groups - 1
    put(last, [choose(last, last % 2, first) for first in range(0, rows, 8)])


def span(count, j):
    return range(count * j // CHUNKS, count * (j + 1) // CHUNKS)


def two_by_two(step, count):
    def body(i, carry):
        step(2 * i, 0)
        step(2 * i + 1, 1)
        return carry

    lax.fori_loop(0, count // 2, body, 0)
    if count % 2:
        step(count - 1, (count - 1) % 2)


def decode(groups, numbers_of, values_of, w_ref, number_ref, high_ref, low_ref, dense_ref, store, unroll):
    rows = dense_ref.shape[1] // TILES
    ids = lax.broadcasted_iota(jnp.int32, (PACK, LANES), 0).astype(jnp.float32)
    ids = [(ids + first).astype(BF) for first in range(0, CH, PACK)]
    zero = jnp.zeros((PACK, LANES), BF)

    def turn(g, buffer):
        number_ref[buffer] = numbers_of(g)
        values = flip(values_of(g))
        high = values.astype(BF).astype(jnp.float32)
        high_ref[buffer] = high
        low_ref[buffer] = values - high

    def row(ref, buffer, s, cell):
        at = s * CELLS + cell
        return jnp.broadcast_to(ref[buffer, at : at + 1, :], (PACK, LANES)).astype(BF)

    def fill(buffer, tiles):
        for t in tiles:
            highs, lows = [], []
            for cell in range(t * PAIR, (t + 1) * PAIR):
                kept = [row(number_ref, buffer, s, cell) for s in range(KEEP)]
                cell_high = [row(high_ref, buffer, s, cell) for s in range(KEEP)]
                cell_low = [row(low_ref, buffer, s, cell) for s in range(KEEP)]
                for some in ids:
                    dense_high, dense_low = zero, zero
                    for s in range(KEEP):
                        hit = kept[s] == some
                        dense_high = jnp.where(hit, cell_high[s], dense_high)
                        dense_low = jnp.where(hit, cell_low[s], dense_low)
                    highs.append(dense_high)
                    lows.append(dense_low)
            here = slice(t * rows, (t + 1) * rows)
            dense_ref[buffer, here, :LANES] = jnp.concatenate(highs, axis=0).T[:rows]
            dense_ref[buffer, here, LANES:] = jnp.concatenate(lows, axis=0).T[:rows]

    def product(g, buffer, tiles):
        parts = [dense_ref[buffer, t * rows : (t + 1) * rows] for t in tiles]
        for t, part in zip(tiles, apply_weights(parts, w_ref[...])):
            store(g, t, part)

    def step(g, buffer):
        turn(g + 1, 1 - buffer)
        for j in range(CHUNKS):
            product(g, buffer, span(TILES, j))
            fill(1 - buffer, span(TILES, j))
        store(g, None, None)

    turn(0, 0)
    fill(0, range(TILES))
    if unroll:
        for g in range(groups - 1):
            step(g, g % 2)
    else:
        two_by_two(step, groups - 1)
    product(groups - 1, (groups - 1) % 2, range(TILES))
    store(groups - 1, None, None)


def side(rep_ref, mine_ref, other_ref, g):
    half = mine_ref.shape[0]
    return jnp.where(g // half == rep_ref[0] % 2, mine_ref[g % half], other_ref[g % half])


def residue_kernel(
    rep_ref, x_ref, chosen_ref, mine_ref, other_ref, w_ref, after_ref, out_hbm, flip_ref,
    number_ref, high_ref, low_ref, dense_ref, out_ref, sem,
):
    groups = x_ref.shape[0]

    def copy(g):
        return pltpu.make_async_copy(out_ref.at[g], out_hbm.at[0, :, columns(g)], sem.at[g])

    def numbers_of(g):
        turned = flip(chosen_ref[g].astype(jnp.float32))
        flip_ref[g] = turned
        return turned

    def store(g, t, part):
        if t is None:
            copy(g).start()
        else:
            here = slice(t * LANES, (t + 1) * LANES)
            out_ref[g, :, here] = x_ref[g, :, here] - part

    decode(
        groups, numbers_of, lambda g: side(rep_ref, mine_ref, other_ref, g), w_ref,
        number_ref, high_ref, low_ref, dense_ref, store, False,
    )
    for g in range(groups):
        copy(g).wait()


def total_kernel(a_ref, b_ref, c_ref, d_ref, after_ref, out_ref):
    out_ref[...] = (a_ref[...] + b_ref[...]) + (c_ref[...] + d_ref[...])


def energy_kernel(replicas, a_ref, b_ref, out_ref, done_ref):
    square = jnp.square(a_ref[...] / replicas) + jnp.square(b_ref[...] / replicas)
    energy = jnp.sum(jnp.sum(square, axis=0, keepdims=True), axis=1, keepdims=True)
    out_ref[...] = jnp.broadcast_to(energy[None], out_ref.shape)
    done_ref[...] = jnp.broadcast_to(energy, done_ref.shape)


def raw_kernel(
    rep_ref, flip_ref, mine_ref, other_ref, w_ref, after_ref, near_ref, far_hbm,
    number_ref, high_ref, low_ref, dense_ref, out_ref, sem,
):
    near = near_ref.shape[0]
    groups = near + out_ref.shape[0]

    def copy(i):
        return pltpu.make_async_copy(out_ref.at[i], far_hbm.at[i], sem.at[i])

    def store(g, t, part):
        far = groups - 1 - g
        if t is None:
            copy(far).start() if g >= near else None
        elif g >= near:
            out_ref[far, :, t * LANES : (t + 1) * LANES] = part
        else:
            near_ref[g, :, t * LANES : (t + 1) * LANES] = part

    decode(
        groups, lambda g: flip_ref[g], lambda g: side(rep_ref, mine_ref, other_ref, g), w_ref,
        number_ref, high_ref, low_ref, dense_ref, store, True,
    )
    for i in range(groups - near):
        copy(i).wait()


def update_kernel(entries, replicas, near_ref, far_hbm, energy_ref, out_hbm, far_ref, out_ref, far_sem, sem):
    groups = out_ref.shape[0]
    near = near_ref.shape[0]

    def fetch(i):
        return pltpu.make_async_copy(far_hbm.at[i], far_ref.at[i], far_sem.at[i])

    def copy(g):
        return pltpu.make_async_copy(out_ref.at[g], out_hbm.at[:, columns(g)], sem.at[g])

    for i in range(groups - near):
        fetch(i).start()
    energy = jnp.sum(energy_ref[:, 0, :], axis=0, keepdims=True)
    scale = lax.rsqrt(energy / entries + 1e-06) / replicas
    scale = jnp.concatenate([scale] * TILES, axis=1)

    def near_body(g, carry):
        out_ref[g] = (near_ref[g] * scale).astype(BF)
        copy(g).start()
        return carry

    def far_body(i, carry):
        fetch(i).wait()
        g = groups - 1 - i
        out_ref[g] = (far_ref[i] * scale).astype(BF)
        copy(g).start()
        return carry

    lax.fori_loop(0, near, near_body, 0)
    lax.fori_loop(0, groups - near, far_body, 0)
    for g in range(groups):
        copy(g).wait()


def call(kernel, name, operands, out_shape, scratch=(), microseconds=1.0):
    specs, arrays = [], []
    for place, array in operands:
        specs.append(pl.BlockSpec(memory_space=place))
        arrays.append(pltpu.with_memory_space_constraint(array, place) if place is pltpu.HBM else array)
    shapes = out_shape if isinstance(out_shape, list) else [out_shape]
    outs = [
        pl.BlockSpec(memory_space=pltpu.HBM if shape.memory_space is pltpu.HBM else pltpu.VMEM)
        for shape in shapes
    ]
    return pl.pallas_call(
        kernel,
        in_specs=specs,
        out_specs=outs if isinstance(out_shape, list) else outs[0],
        out_shape=out_shape,
        scratch_shapes=list(scratch),
        compiler_params=pltpu.CompilerParams(vmem_limit_bytes=VMEM_BYTES),
        cost_estimate=pl.CostEstimate(
            flops=0, bytes_accessed=int(microseconds * 3.0e6), transcendentals=0
        ),
        name=name,
    )(*arrays)


def per_device(momentum, kept, counts):
    _, rows, width = momentum.shape
    blocks = width // CH
    groups = width // WIDTH
    half = groups // 2
    replicas = lax.axis_size("rep")
    shards = lax.axis_size("fsdp")
    rep = lax.axis_index("rep").astype(jnp.int32).reshape(1)
    basis = pair_table()
    forward = jnp.asarray(split_weights(basis.T))
    inverse = jnp.asarray(split_weights(basis))
    hbm, vmem, smem = pltpu.HBM, pltpu.VMEM, pltpu.SMEM
    half_shape = (half, rows, LANES)
    flat = (half * rows, LANES)
    dma = pltpu.SemaphoreType.DMA
    turned = [vmem((2, LANES, LANES), jnp.float32)] * 3 + [vmem((2, TILES * rows, 2 * LANES), BF)]

    numbers, mine, other, x = call(
        pick_kernel,
        "pick",
        [
            (smem, rep),
            (hbm, momentum),
            (hbm, jnp.transpose(kept, (0, 2, 1))),
            (hbm, counts),
            (hbm, forward),
        ],
        [
            vmem((groups, rows, LANES), jnp.int32),
            vmem(half_shape, jnp.float32),
            vmem(half_shape, jnp.float32),
            vmem((groups, rows, WIDTH), jnp.float32),
        ],
        [
            vmem((rows, KEEP, blocks), jnp.int32),
            vmem((rows, blocks), jnp.int32),
            vmem(forward.shape, BF),
            vmem((groups, rows, LANES), jnp.float32),
            vmem((2, TILES, rows, LANES), jnp.float32),
            dma((3,)),
            dma((groups,)),
        ],
        5.0,
    )

    swap = [(i, i ^ 1) for i in range(replicas)]
    chip = mine.reshape(flat) + lax.ppermute(other.reshape(flat), "rep", swap)
    away = []
    for step in (4, 2, 6):
        ring = [(i, (i + step) % replicas) for i in range(replicas)]
        away.append(lax.ppermute(chip, "rep", ring))
    new_moment, flipped = call(
        residue_kernel,
        "residue",
        [
            (smem, rep),
            (vmem, x),
            (vmem, numbers),
            (vmem, mine),
            (vmem, other),
            (vmem, inverse),
            (vmem, chip),
        ],
        [hbm(momentum.shape, jnp.float32), vmem((groups, LANES, LANES), jnp.float32)],
        turned + [vmem((groups, rows, WIDTH), jnp.float32), dma((groups,))],
        5.0,
    )
    total = call(
        total_kernel,
        "total",
        [(vmem, chip)] + [(vmem, part) for part in away] + [(vmem, flipped)],
        vmem(flat, jnp.float32),
        microseconds=0.5,
    )
    total_other = lax.ppermute(total, "rep", swap)
    own_energy, done = call(
        functools.partial(energy_kernel, replicas),
        "energy",
        [(vmem, total), (vmem, total_other)],
        [vmem((shards, 1, LANES), jnp.float32), vmem((8, LANES), jnp.float32)],
        microseconds=0.5,
    )
    energies = lax.all_to_all(own_energy, "fsdp", 0, 0, tiled=True)
    far = groups - half
    near_raw, far_raw = call(
        raw_kernel,
        "raw",
        [
            (smem, rep),
            (vmem, flipped),
            (vmem, total.reshape(half_shape)),
            (vmem, total_other.reshape(half_shape)),
            (vmem, inverse),
            (vmem, done),
        ],
        [vmem((half, rows, WIDTH), jnp.float32), hbm((far, rows, WIDTH), jnp.float32)],
        turned + [vmem((far, rows, WIDTH), jnp.float32), dma((far,))],
        5.0,
    )
    update = call(
        functools.partial(update_kernel, rows * width * shards, replicas),
        "update",
        [(vmem, near_raw), (hbm, far_raw), (vmem, energies)],
        hbm((rows, width), BF),
        [vmem((far, rows, WIDTH), jnp.float32), vmem((groups, rows, WIDTH), BF), dma((far,)), dma((groups,))],
        2.0,
    )
    return new_moment, update


def solution(mesh):
    placed = (P("rep", "fsdp", None), P("fsdp", None, None), P(None, "fsdp", None))
    return jax.shard_map(
        per_device,
        mesh=mesh,
        in_specs=placed,
        out_specs=(P("rep", "fsdp", None), P("fsdp", None)),
        check_vma=False,
    )
```

```python
import functools
import math

import jax
import jax.numpy as jnp
import ml_dtypes
import numpy as np
from jax import lax
from jax.experimental import pallas as pl
from jax.experimental.pallas import tpu as pltpu
from jax.sharding import PartitionSpec as P

CH = 64
KEEP = 4
LANES = 128
PACK = 16
PAIR = LANES // CH
CELLS = LANES // KEEP
TILES = CELLS // PAIR
WIDTH = TILES * LANES
BF = jnp.bfloat16
VMEM_BYTES = 32 << 20
CHUNKS = 4


def pair_table():
    k, n = np.arange(CH)[:, None], np.arange(CH)[None, :]
    basis = np.cos(math.pi * (2 * n + 1) * k / (2 * CH)) * math.sqrt(2 / CH)
    basis[0] = math.sqrt(1 / CH)
    return np.kron(np.eye(PAIR), basis)


def split_weights(table):
    high = table.astype(ml_dtypes.bfloat16)
    low = (table - high.astype(np.float64)).astype(ml_dtypes.bfloat16)
    side = np.concatenate([high, low], axis=1)
    return np.concatenate([side, side], axis=0)


def halves(x):
    high = x.astype(BF)
    return high, (x - high.astype(jnp.float32)).astype(BF)


def apply_weights(tiles, weights):
    rows = tiles[0].shape[0]
    out = jnp.dot(jnp.concatenate(tiles, axis=0), weights, preferred_element_type=jnp.float32)
    out = out[:, :LANES] + out[:, LANES:]
    return [out[i * rows : (i + 1) * rows] for i in range(len(tiles))]


def lane_gather(x, index):
    return jnp.take_along_axis(x, index, axis=1, mode="promise_in_bounds")


def lane_ids(rows):
    return lax.broadcasted_iota(jnp.int32, (rows, LANES), 1)


def spread(value, group, rows):
    start = group * CELLS
    base = start // LANES * LANES
    part = value[:, base : base + LANES]
    if part.shape[1] < LANES:
        part = jnp.pad(part, ((0, 0), (0, LANES - part.shape[1])))
    return lane_gather(part, start - base + lane_ids(rows) % CELLS)


def flip(x):
    fill = LANES - x.shape[0]
    return jnp.concatenate([x, x[:fill]], axis=0).T if fill else x.T


def columns(group):
    return pl.ds(pl.multiple_of(group * WIDTH, WIDTH), WIDTH)


def choose_groups(x_ref, number_ref, live_ref, w_ref, coeff_ref, out_ref, first_group):
    count, rows, _ = out_ref.shape
    lanes = lane_ids(8)
    block_start = lanes % PAIR * CH
    tile_of = lanes % CELLS // PAIR

    def transform(i, buffer, tiles):
        g = first_group + i
        parts = [
            jnp.concatenate(halves(x_ref[g, :, t * LANES : (t + 1) * LANES]), axis=1) for t in tiles
        ]
        for t, coeffs in zip(tiles, apply_weights(parts, w_ref[...])):
            coeff_ref[buffer, t] = coeffs

    def choose(i, buffer, first):
        here = slice(first, first + 8)
        index = number_ref[first_group + i, here] + block_start
        picked = jnp.zeros((8, LANES), jnp.float32)
        for t in range(TILES):
            picked = jnp.where(tile_of == t, lane_gather(coeff_ref[buffer, t, here], index), picked)
        out_ref[i, here] = jnp.where(live_ref[first_group + i, here] > 0.0, picked, 0.0)

    transform(0, 0, range(TILES))
    for i in range(count - 1):
        for j in range(CHUNKS):
            transform(i + 1, (i + 1) % 2, span(TILES, j))
            for part in span(rows // 8, j):
                choose(i, i % 2, 8 * part)
    for part in range(rows // 8):
        choose(count - 1, (count - 1) % 2, 8 * part)


def pick_other_kernel(
    rep_ref, x_hbm, kept_hbm, cnt_hbm, w_hbm, number_ref, live_ref, other_ref, x_ref,
    kept_ref, cnt_ref, w_ref, coeff_ref, small_sem, x_sem,
):
    groups, rows, _ = x_ref.shape
    half = groups // 2
    core = rep_ref[0] % 2
    theirs, ours = (1 - core) * half, core * half
    small = [
        pltpu.make_async_copy(w_hbm, w_ref, small_sem.at[0]),
        pltpu.make_async_copy(kept_hbm, kept_ref, small_sem.at[1]),
        pltpu.make_async_copy(cnt_hbm.at[rep_ref[0]], cnt_ref, small_sem.at[2]),
    ]
    for copy in small:
        copy.start()

    def x_copy(first, i):
        g = first + i
        return pltpu.make_async_copy(x_hbm.at[0, :, columns(g)], x_ref.at[g], x_sem.at[g])

    for i in range(half):
        x_copy(theirs, i).start()
    for copy in small:
        copy.wait()
    for i in range(half):
        x_copy(theirs, i).wait()
    for i in range(half):
        x_copy(ours, i).start()

    slot = lane_ids(rows) // CELLS
    counts = cnt_ref[...]
    numbers = [kept_ref[:, s, :] for s in range(KEEP)]
    for g in range(groups):
        chosen = spread(numbers[0], g, rows)
        for s in range(1, KEEP):
            chosen = jnp.where(slot == s, spread(numbers[s], g, rows), chosen)
        number_ref[g] = chosen
        live_ref[g] = jnp.where(slot < spread(counts, g, rows), 1.0, 0.0)

    choose_groups(x_ref, number_ref, live_ref, w_ref, coeff_ref, other_ref, theirs)
    for i in range(half):
        x_copy(ours, i).wait()


def pick_mine_kernel(rep_ref, x_ref, number_ref, live_ref, w_ref, mine_ref, coeff_ref):
    first = rep_ref[0] % 2 * mine_ref.shape[0]
    choose_groups(x_ref, number_ref, live_ref, w_ref, coeff_ref, mine_ref, first)


def span(count, j):
    return range(count * j // CHUNKS, count * (j + 1) // CHUNKS)


def two_by_two(step, count):
    def body(i, carry):
        step(2 * i, 0)
        step(2 * i + 1, 1)
        return carry

    lax.fori_loop(0, count // 2, body, 0)
    if count % 2:
        step(count - 1, (count - 1) % 2)


def decode(groups, numbers_of, values_of, w_ref, number_ref, high_ref, low_ref, dense_ref, store, unroll):
    rows = dense_ref.shape[1] // TILES
    ids = lax.broadcasted_iota(jnp.int32, (PACK, LANES), 0).astype(jnp.float32)
    ids = [(ids + first).astype(BF) for first in range(0, CH, PACK)]
    zero = jnp.zeros((PACK, LANES), BF)

    def turn(g, buffer):
        number_ref[buffer] = numbers_of(g)
        values = flip(values_of(g))
        high = values.astype(BF).astype(jnp.float32)
        high_ref[buffer] = high
        low_ref[buffer] = values - high

    def row(ref, buffer, s, cell):
        at = s * CELLS + cell
        return jnp.broadcast_to(ref[buffer, at : at + 1, :], (PACK, LANES)).astype(BF)

    def fill(buffer, tiles):
        for t in tiles:
            highs, lows = [], []
            for cell in range(t * PAIR, (t + 1) * PAIR):
                kept = [row(number_ref, buffer, s, cell) for s in range(KEEP)]
                cell_high = [row(high_ref, buffer, s, cell) for s in range(KEEP)]
                cell_low = [row(low_ref, buffer, s, cell) for s in range(KEEP)]
                for some in ids:
                    dense_high, dense_low = zero, zero
                    for s in range(KEEP):
                        hit = kept[s] == some
                        dense_high = jnp.where(hit, cell_high[s], dense_high)
                        dense_low = jnp.where(hit, cell_low[s], dense_low)
                    highs.append(dense_high)
                    lows.append(dense_low)
            here = slice(t * rows, (t + 1) * rows)
            dense_ref[buffer, here, :LANES] = jnp.concatenate(highs, axis=0).T[:rows]
            dense_ref[buffer, here, LANES:] = jnp.concatenate(lows, axis=0).T[:rows]

    def product(g, buffer, tiles):
        parts = [dense_ref[buffer, t * rows : (t + 1) * rows] for t in tiles]
        for t, part in zip(tiles, apply_weights(parts, w_ref[...])):
            store(g, t, part)

    def step(g, buffer):
        turn(g + 1, 1 - buffer)
        for j in range(CHUNKS):
            product(g, buffer, span(TILES, j))
            fill(1 - buffer, span(TILES, j))
        store(g, None, None)

    turn(0, 0)
    fill(0, range(TILES))
    if unroll:
        for g in range(groups - 1):
            step(g, g % 2)
    else:
        two_by_two(step, groups - 1)
    product(groups - 1, (groups - 1) % 2, range(TILES))
    store(groups - 1, None, None)


def side(rep_ref, mine_ref, other_ref, g):
    half = mine_ref.shape[0]
    return jnp.where(g // half == rep_ref[0] % 2, mine_ref[g % half], other_ref[g % half])


def residue_kernel(
    first, rep_ref, x_ref, chosen_ref, mine_ref, other_ref, w_ref, after_ref, *refs
):
    (
        out_hbm, flip_hbm, done_ref, number_ref, high_ref, low_ref, dense_ref, out_ref, flip_ref, sem, flip_sem,
    ) = refs[-11:]
    count = out_ref.shape[0]
    done_ref[...] = jnp.zeros(done_ref.shape, jnp.float32)

    def copy(i):
        return pltpu.make_async_copy(out_ref.at[i], out_hbm.at[0, :, columns(first + i)], sem.at[i])

    def flip_copy(i):
        return pltpu.make_async_copy(flip_ref.at[i], flip_hbm.at[i], flip_sem.at[i])

    def numbers_of(i):
        turned = flip(chosen_ref[first + i].astype(jnp.float32))
        flip_ref[i] = turned
        flip_copy(i).start()
        return turned

    def store(i, t, part):
        if t is None:
            copy(i).start()
        else:
            here = slice(t * LANES, (t + 1) * LANES)
            out_ref[i, :, here] = x_ref[first + i, :, here] - part

    decode(
        count, numbers_of, lambda i: side(rep_ref, mine_ref, other_ref, first + i), w_ref,
        number_ref, high_ref, low_ref, dense_ref, store, False,
    )
    for i in range(count):
        copy(i).wait()
        flip_copy(i).wait()


def add_kernel(*refs, counts):
    refs = list(refs)
    left, right = [[refs.pop(0) for _ in range(count)] for count in counts[:2]]
    outs = refs[len(refs) - counts[2] :]
    left, right = [jnp.concatenate([ref[...] for ref in part], axis=0) for part in (left, right)]
    total = left + right
    at = 0
    for out in outs:
        out[...] = total[at : at + out.shape[0]]
        at += out.shape[0]


def energy_kernel(replicas, a_ref, b_ref, out_ref, done_ref):
    square = jnp.square(a_ref[...] / replicas) + jnp.square(b_ref[...] / replicas)
    energy = jnp.sum(jnp.sum(square, axis=0, keepdims=True), axis=1, keepdims=True)
    out_ref[...] = jnp.broadcast_to(energy[None], out_ref.shape)
    done_ref[...] = jnp.broadcast_to(energy, done_ref.shape)


def raw_kernel(
    rep_ref, low_flip_hbm, high_flip_hbm, mine_ref, other_ref, w_hbm, after_ref, near_ref, far_hbm,
    number_ref, high_ref, low_ref, dense_ref, out_ref, flip_ref, w_ref, sem, in_sem,
):
    near = near_ref.shape[0]
    groups = near + out_ref.shape[0]
    fetches = [
        pltpu.make_async_copy(low_flip_hbm, flip_ref.at[: groups // 2], in_sem.at[0]),
        pltpu.make_async_copy(high_flip_hbm, flip_ref.at[groups // 2 :], in_sem.at[1]),
        pltpu.make_async_copy(w_hbm, w_ref, in_sem.at[2]),
    ]
    for fetch in fetches:
        fetch.start()
    for fetch in fetches:
        fetch.wait()

    def copy(i):
        return pltpu.make_async_copy(out_ref.at[i], far_hbm.at[i], sem.at[i])

    def store(g, t, part):
        far = groups - 1 - g
        if t is None:
            copy(far).start() if g >= near else None
        elif g >= near:
            out_ref[far, :, t * LANES : (t + 1) * LANES] = part
        else:
            near_ref[g, :, t * LANES : (t + 1) * LANES] = part

    decode(
        groups, lambda g: flip_ref[g], lambda g: side(rep_ref, mine_ref, other_ref, g), w_ref,
        number_ref, high_ref, low_ref, dense_ref, store, True,
    )
    for i in range(groups - near):
        copy(i).wait()


def update_kernel(entries, replicas, near_ref, far_hbm, energy_ref, out_hbm, far_ref, out_ref, far_sem, sem):
    groups = out_ref.shape[0]
    near = near_ref.shape[0]

    def fetch(i):
        return pltpu.make_async_copy(far_hbm.at[i], far_ref.at[i], far_sem.at[i])

    def copy(g):
        return pltpu.make_async_copy(out_ref.at[g], out_hbm.at[:, columns(g)], sem.at[g])

    for i in range(groups - near):
        fetch(i).start()
    energy = jnp.sum(energy_ref[:, 0, :], axis=0, keepdims=True)
    scale = lax.rsqrt(energy / entries + 1e-06) / replicas
    scale = jnp.concatenate([scale] * TILES, axis=1)

    def near_body(g, carry):
        out_ref[g] = (near_ref[g] * scale).astype(BF)
        copy(g).start()
        return carry

    def far_body(i, carry):
        fetch(i).wait()
        g = groups - 1 - i
        out_ref[g] = (far_ref[i] * scale).astype(BF)
        copy(g).start()
        return carry

    lax.fori_loop(0, near, near_body, 0)
    lax.fori_loop(0, groups - near, far_body, 0)
    for g in range(groups):
        copy(g).wait()


def call(kernel, name, operands, out_shape, scratch=(), microseconds=1.0, aliases=()):
    specs, arrays = [], []
    for place, array in operands:
        specs.append(pl.BlockSpec(memory_space=place))
        arrays.append(pltpu.with_memory_space_constraint(array, place) if place is pltpu.HBM else array)
    shapes = out_shape if isinstance(out_shape, list) else [out_shape]
    outs = [
        pl.BlockSpec(memory_space=pltpu.HBM if shape.memory_space is pltpu.HBM else pltpu.VMEM)
        for shape in shapes
    ]
    return pl.pallas_call(
        kernel,
        in_specs=specs,
        out_specs=outs if isinstance(out_shape, list) else outs[0],
        out_shape=out_shape,
        scratch_shapes=list(scratch),
        input_output_aliases=dict(aliases),
        compiler_params=pltpu.CompilerParams(vmem_limit_bytes=VMEM_BYTES),
        cost_estimate=pl.CostEstimate(
            flops=0, bytes_accessed=int(microseconds * 3.0e6), transcendentals=0
        ),
        name=name,
    )(*arrays)


def per_device(momentum, kept, counts):
    _, rows, width = momentum.shape
    blocks = width // CH
    groups = width // WIDTH
    half = groups // 2
    replicas = lax.axis_size("rep")
    shards = lax.axis_size("fsdp")
    rep = lax.axis_index("rep").astype(jnp.int32).reshape(1)
    basis = pair_table()
    forward = jnp.asarray(split_weights(basis.T))
    inverse = jnp.asarray(split_weights(basis))
    hbm, vmem, smem = pltpu.HBM, pltpu.VMEM, pltpu.SMEM
    half_shape = (half, rows, LANES)
    flat = (half * rows, LANES)
    dma = pltpu.SemaphoreType.DMA
    turned = [vmem((2, LANES, LANES), jnp.float32)] * 3 + [vmem((2, TILES * rows, 2 * LANES), BF)]

    coeffs = vmem((2, TILES, rows, LANES), jnp.float32)

    numbers, live, other, x = call(
        pick_other_kernel,
        "pick_other",
        [
            (smem, rep),
            (hbm, momentum),
            (hbm, jnp.transpose(kept, (0, 2, 1))),
            (hbm, counts),
            (hbm, forward),
        ],
        [
            vmem((groups, rows, LANES), jnp.int32),
            vmem((groups, rows, LANES), jnp.float32),
            vmem(half_shape, jnp.float32),
            vmem((groups, rows, WIDTH), jnp.float32),
        ],
        [
            vmem((rows, KEEP, blocks), jnp.int32),
            vmem((rows, blocks), jnp.int32),
            vmem(forward.shape, BF),
            coeffs,
            dma((3,)),
            dma((groups,)),
        ],
        4.0,
    )
    mine = call(
        pick_mine_kernel,
        "pick_mine",
        [(smem, rep), (vmem, x), (vmem, numbers), (vmem, live), (vmem, forward)],
        vmem(half_shape, jnp.float32),
        [coeffs],
        2.0,
    )

    swap = [(i, i ^ 1) for i in range(replicas)]
    pieces = 1
    piece = vmem((flat[0] // pieces, LANES), jnp.float32)

    def add(name, left, right, after, out):
        counts = (len(left), len(right), len(out))
        return list(
            call(
                functools.partial(add_kernel, counts=counts),
                name,
                [(vmem, array) for array in left + right + after],
                out,
                microseconds=0.3,
            )
        )

    partner = lax.ppermute(other.reshape(flat), "rep", swap)
    total = add("chip", [mine.reshape(flat)], [partner], [], [piece] * pieces)
    new_moment = None
    flips = []
    for part in range(2):
        pairs = []
        for y in range(replicas // 2):
            for core in range(2):
                there = y ^ 1 if part == core else (y + (1 if y % 2 else -1)) % (replicas // 2)
                pairs.append((2 * y + core, 2 * there + core))
        arrived = [lax.ppermute(some, "rep", pairs) for some in total]
        earlier = [] if new_moment is None else [(hbm, new_moment)]
        new_moment, flipped, done = call(
            functools.partial(residue_kernel, part * half),
            f"residue_{part}",
            [
                (smem, rep),
                (vmem, x),
                (vmem, numbers),
                (vmem, mine),
                (vmem, other),
                (vmem, inverse),
                (vmem, total[0]),
            ]
            + earlier,
            [
                hbm(momentum.shape, jnp.float32),
                hbm((half, LANES, LANES), jnp.float32),
                vmem((8, LANES), jnp.float32),
            ],
            turned
            + [
                vmem((half, rows, WIDTH), jnp.float32),
                vmem((half, LANES, LANES), jnp.float32),
                dma((half,)),
                dma((half,)),
            ],
            2.5,
            {7: 0} if earlier else {},
        )
        flips.append(flipped)
        out = [vmem(flat, jnp.float32)] if part else [piece] * pieces
        total = add(f"sum_{part}", total, arrived, [done], out)
    (total,) = total
    total_other = lax.ppermute(total, "rep", swap)
    own_energy, summed = call(
        functools.partial(energy_kernel, replicas),
        "energy",
        [(vmem, total), (vmem, total_other)],
        [vmem((shards, 1, LANES), jnp.float32), vmem((8, LANES), jnp.float32)],
        microseconds=0.5,
    )
    energies = lax.all_to_all(own_energy, "fsdp", 0, 0, tiled=True)
    near = groups * 2 // 3
    far = groups - near
    near_raw, far_raw = call(
        raw_kernel,
        "raw",
        [
            (smem, rep),
            (hbm, flips[0]),
            (hbm, flips[1]),
            (vmem, total.reshape(half_shape)),
            (vmem, total_other.reshape(half_shape)),
            (hbm, inverse),
            (vmem, summed),
        ],
        [vmem((near, rows, WIDTH), jnp.float32), hbm((far, rows, WIDTH), jnp.float32)],
        turned
        + [
            vmem((far, rows, WIDTH), jnp.float32),
            vmem((groups, LANES, LANES), jnp.float32),
            vmem(inverse.shape, BF),
            dma((far,)),
            dma((3,)),
        ],
        5.0,
    )
    update = call(
        functools.partial(update_kernel, rows * width * shards, replicas),
        "update",
        [(vmem, near_raw), (hbm, far_raw), (vmem, energies)],
        hbm((rows, width), BF),
        [vmem((far, rows, WIDTH), jnp.float32), vmem((groups, rows, WIDTH), BF), dma((far,)), dma((groups,))],
        2.0,
    )
    return new_moment, update


def solution(mesh):
    placed = (P("rep", "fsdp", None), P("fsdp", None, None), P(None, "fsdp", None))
    return jax.shard_map(
        per_device,
        mesh=mesh,
        in_specs=placed,
        out_specs=(P("rep", "fsdp", None), P("fsdp", None)),
        check_vma=False,
    )
```

```python
import functools
import math

import jax
import jax.numpy as jnp
import ml_dtypes
import numpy as np
from jax import lax
from jax.experimental import pallas as pl
from jax.experimental.pallas import tpu as pltpu
from jax.sharding import Mesh, PartitionSpec as P

CH = 64
KEEP = 4
LANES = 128
PACK = 16
PAIR = LANES // CH
CELLS = LANES // KEEP
TILES = CELLS // PAIR
WIDTH = TILES * LANES
BF = jnp.bfloat16
REP = ("y", "core")
FSDP = ("z", "x")
VMEM_BYTES = 32 << 20
CHUNKS = 4


def pair_table():
    k, n = np.arange(CH)[:, None], np.arange(CH)[None, :]
    basis = np.cos(math.pi * (2 * n + 1) * k / (2 * CH)) * math.sqrt(2 / CH)
    basis[0] = math.sqrt(1 / CH)
    return np.kron(np.eye(PAIR), basis)


def split_weights(table):
    high = table.astype(ml_dtypes.bfloat16)
    low = (table - high.astype(np.float64)).astype(ml_dtypes.bfloat16)
    side = np.concatenate([high, low], axis=1)
    return np.concatenate([side, side], axis=0)


def halves(x):
    high = x.astype(BF)
    return high, (x - high.astype(jnp.float32)).astype(BF)


def apply_weights(tiles, weights):
    rows = tiles[0].shape[0]
    out = jnp.dot(jnp.concatenate(tiles, axis=0), weights, preferred_element_type=jnp.float32)
    out = out[:, :LANES] + out[:, LANES:]
    return [out[i * rows : (i + 1) * rows] for i in range(len(tiles))]


def lane_gather(x, index):
    return jnp.take_along_axis(x, index, axis=1, mode="promise_in_bounds")


def lane_ids(rows):
    return lax.broadcasted_iota(jnp.int32, (rows, LANES), 1)


def spread(value, group, rows):
    start = group * CELLS
    base = start // LANES * LANES
    part = value[:, base : base + LANES]
    if part.shape[1] < LANES:
        part = jnp.pad(part, ((0, 0), (0, LANES - part.shape[1])))
    return lane_gather(part, start - base + lane_ids(rows) % CELLS)


def flip(x):
    fill = LANES - x.shape[0]
    return jnp.concatenate([x, x[:fill]], axis=0).T if fill else x.T


def columns(group):
    return pl.ds(pl.multiple_of(group * WIDTH, WIDTH), WIDTH)


def choose_groups(x_ref, number_ref, live_ref, w_ref, coeff_ref, out_ref, first_group):
    count, rows, _ = out_ref.shape
    lanes = lane_ids(8)
    block_start = lanes % PAIR * CH
    tile_of = lanes % CELLS // PAIR

    def transform(i, buffer, tiles):
        g = first_group + i
        parts = [
            jnp.concatenate(halves(x_ref[g, :, t * LANES : (t + 1) * LANES]), axis=1) for t in tiles
        ]
        for t, coeffs in zip(tiles, apply_weights(parts, w_ref[...])):
            coeff_ref[buffer, t] = coeffs

    def choose(i, buffer, first):
        here = slice(first, first + 8)
        index = number_ref[first_group + i, here] + block_start
        picked = jnp.zeros((8, LANES), jnp.float32)
        for t in range(TILES):
            picked = jnp.where(tile_of == t, lane_gather(coeff_ref[buffer, t, here], index), picked)
        out_ref[i, here] = jnp.where(live_ref[first_group + i, here] > 0.0, picked, 0.0)

    transform(0, 0, range(TILES))
    for i in range(count - 1):
        for j in range(CHUNKS):
            transform(i + 1, (i + 1) % 2, span(TILES, j))
            for part in span(rows // 8, j):
                choose(i, i % 2, 8 * part)
    for part in range(rows // 8):
        choose(count - 1, (count - 1) % 2, 8 * part)


def pick_other_kernel(
    rep_ref, x_hbm, kept_hbm, cnt_hbm, w_hbm, number_ref, live_ref, other_ref, x_ref,
    kept_ref, cnt_ref, w_ref, coeff_ref, small_sem, x_sem,
):
    groups, rows, _ = x_ref.shape
    half = groups // 2
    core = rep_ref[0] % 2
    theirs, ours = (1 - core) * half, core * half
    small = [
        pltpu.make_async_copy(w_hbm, w_ref, small_sem.at[0]),
        pltpu.make_async_copy(kept_hbm, kept_ref, small_sem.at[1]),
        pltpu.make_async_copy(cnt_hbm.at[rep_ref[0]], cnt_ref, small_sem.at[2]),
    ]
    for copy in small:
        copy.start()

    def x_copy(first, i):
        g = first + i
        return pltpu.make_async_copy(x_hbm.at[0, :, columns(g)], x_ref.at[g], x_sem.at[g])

    for i in range(half):
        x_copy(theirs, i).start()
    for copy in small:
        copy.wait()
    for i in range(half):
        x_copy(theirs, i).wait()
    for i in range(half):
        x_copy(ours, i).start()

    slot = lane_ids(rows) // CELLS
    counts = cnt_ref[...]
    numbers = [kept_ref[:, s, :] for s in range(KEEP)]
    for g in range(groups):
        chosen = spread(numbers[0], g, rows)
        for s in range(1, KEEP):
            chosen = jnp.where(slot == s, spread(numbers[s], g, rows), chosen)
        number_ref[g] = chosen
        live_ref[g] = jnp.where(slot < spread(counts, g, rows), 1.0, 0.0)

    choose_groups(x_ref, number_ref, live_ref, w_ref, coeff_ref, other_ref, theirs)
    for i in range(half):
        x_copy(ours, i).wait()


def pick_mine_kernel(rep_ref, x_ref, number_ref, live_ref, w_ref, mine_ref, coeff_ref):
    first = rep_ref[0] % 2 * mine_ref.shape[0]
    choose_groups(x_ref, number_ref, live_ref, w_ref, coeff_ref, mine_ref, first)


def span(count, j):
    return range(count * j // CHUNKS, count * (j + 1) // CHUNKS)


def two_by_two(step, count):
    def body(i, carry):
        step(2 * i, 0)
        step(2 * i + 1, 1)
        return carry

    lax.fori_loop(0, count // 2, body, 0)
    if count % 2:
        step(count - 1, (count - 1) % 2)


def decode(groups, numbers_of, values_of, w_ref, number_ref, high_ref, low_ref, dense_ref, store, unroll):
    rows = dense_ref.shape[1] // TILES
    ids = lax.broadcasted_iota(jnp.int32, (PACK, LANES), 0).astype(jnp.float32)
    ids = [(ids + first).astype(BF) for first in range(0, CH, PACK)]
    zero = jnp.zeros((PACK, LANES), BF)

    def turn(g, buffer):
        number_ref[buffer] = numbers_of(g)
        values = flip(values_of(g))
        high = values.astype(BF).astype(jnp.float32)
        high_ref[buffer] = high
        low_ref[buffer] = values - high

    def row(ref, buffer, s, cell):
        at = s * CELLS + cell
        return jnp.broadcast_to(ref[buffer, at : at + 1, :], (PACK, LANES)).astype(BF)

    def fill(buffer, tiles):
        for t in tiles:
            highs, lows = [], []
            for cell in range(t * PAIR, (t + 1) * PAIR):
                kept = [row(number_ref, buffer, s, cell) for s in range(KEEP)]
                cell_high = [row(high_ref, buffer, s, cell) for s in range(KEEP)]
                cell_low = [row(low_ref, buffer, s, cell) for s in range(KEEP)]
                for some in ids:
                    dense_high, dense_low = zero, zero
                    for s in range(KEEP):
                        hit = kept[s] == some
                        dense_high = jnp.where(hit, cell_high[s], dense_high)
                        dense_low = jnp.where(hit, cell_low[s], dense_low)
                    highs.append(dense_high)
                    lows.append(dense_low)
            here = slice(t * rows, (t + 1) * rows)
            dense_ref[buffer, here, :LANES] = jnp.concatenate(highs, axis=0).T[:rows]
            dense_ref[buffer, here, LANES:] = jnp.concatenate(lows, axis=0).T[:rows]

    def product(g, buffer, tiles):
        parts = [dense_ref[buffer, t * rows : (t + 1) * rows] for t in tiles]
        for t, part in zip(tiles, apply_weights(parts, w_ref[...])):
            store(g, t, part)

    def step(g, buffer):
        turn(g + 1, 1 - buffer)
        for j in range(CHUNKS):
            product(g, buffer, span(TILES, j))
            fill(1 - buffer, span(TILES, j))
        store(g, None, None)

    turn(0, 0)
    fill(0, range(TILES))
    if unroll:
        for g in range(groups - 1):
            step(g, g % 2)
    else:
        two_by_two(step, groups - 1)
    product(groups - 1, (groups - 1) % 2, range(TILES))
    store(groups - 1, None, None)


def side(rep_ref, mine_ref, other_ref, g):
    half = mine_ref.shape[0]
    return jnp.where(g // half == rep_ref[0] % 2, mine_ref[g % half], other_ref[g % half])


def residue_kernel(
    first, rep_ref, x_ref, chosen_ref, mine_ref, other_ref, w_ref, after_ref, *refs
):
    (
        out_hbm, flip_hbm, done_ref, number_ref, high_ref, low_ref, dense_ref, out_ref, flip_ref, sem, flip_sem,
    ) = refs[-11:]
    count = out_ref.shape[0]
    done_ref[...] = jnp.zeros(done_ref.shape, jnp.float32)

    def copy(i):
        return pltpu.make_async_copy(out_ref.at[i], out_hbm.at[0, :, columns(first + i)], sem.at[i])

    def flip_copy(i):
        return pltpu.make_async_copy(flip_ref.at[i], flip_hbm.at[i], flip_sem.at[i])

    def numbers_of(i):
        turned = flip(chosen_ref[first + i].astype(jnp.float32))
        flip_ref[i] = turned
        flip_copy(i).start()
        return turned

    def store(i, t, part):
        if t is None:
            copy(i).start()
        else:
            here = slice(t * LANES, (t + 1) * LANES)
            out_ref[i, :, here] = x_ref[first + i, :, here] - part

    decode(
        count, numbers_of, lambda i: side(rep_ref, mine_ref, other_ref, first + i), w_ref,
        number_ref, high_ref, low_ref, dense_ref, store, False,
    )
    for i in range(count):
        copy(i).wait()
        flip_copy(i).wait()


def add_kernel(*refs, counts):
    refs = list(refs)
    left, right = [[refs.pop(0) for _ in range(count)] for count in counts[:2]]
    outs = refs[len(refs) - counts[2] :]
    left, right = [jnp.concatenate([ref[...] for ref in part], axis=0) for part in (left, right)]
    total = left + right
    at = 0
    for out in outs:
        out[...] = total[at : at + out.shape[0]]
        at += out.shape[0]


def energy_kernel(replicas, total_ref, out_ref, total_out_ref):
    total = total_ref[...]
    total_out_ref[...] = total
    square = jnp.square(total / replicas)
    energy = jnp.sum(jnp.sum(square, axis=0, keepdims=True), axis=1, keepdims=True)
    out_ref[...] = jnp.broadcast_to(energy[None], out_ref.shape)


def raw_kernel(
    rep_ref, low_flip_hbm, high_flip_hbm, mine_ref, other_ref, w_hbm, near_ref, far_hbm,
    number_ref, high_ref, low_ref, dense_ref, out_ref, flip_ref, w_ref, sem, in_sem,
):
    near = near_ref.shape[0]
    groups = near + out_ref.shape[0]
    fetches = [
        pltpu.make_async_copy(low_flip_hbm, flip_ref.at[: groups // 2], in_sem.at[0]),
        pltpu.make_async_copy(high_flip_hbm, flip_ref.at[groups // 2 :], in_sem.at[1]),
        pltpu.make_async_copy(w_hbm, w_ref, in_sem.at[2]),
    ]
    for fetch in fetches:
        fetch.start()
    for fetch in fetches:
        fetch.wait()

    def copy(i):
        return pltpu.make_async_copy(out_ref.at[i], far_hbm.at[i], sem.at[i])

    def store(g, t, part):
        far = groups - 1 - g
        if t is None:
            copy(far).start() if g >= near else None
        elif g >= near:
            out_ref[far, :, t * LANES : (t + 1) * LANES] = part
        else:
            near_ref[g, :, t * LANES : (t + 1) * LANES] = part

    decode(
        groups, lambda g: flip_ref[g], lambda g: side(rep_ref, mine_ref, other_ref, g), w_ref,
        number_ref, high_ref, low_ref, dense_ref, store, True,
    )
    for i in range(groups - near):
        copy(i).wait()


def update_kernel(entries, replicas, near_ref, far_hbm, energy_ref, out_hbm, far_ref, out_ref, far_sem, sem):
    groups = out_ref.shape[0]
    near = near_ref.shape[0]

    def fetch(i):
        return pltpu.make_async_copy(far_hbm.at[i], far_ref.at[i], far_sem.at[i])

    def copy(g):
        return pltpu.make_async_copy(out_ref.at[g], out_hbm.at[:, columns(g)], sem.at[g])

    for i in range(groups - near):
        fetch(i).start()
    energy = jnp.sum(energy_ref[:, 0, :], axis=0, keepdims=True)
    scale = lax.rsqrt(energy / entries + 1e-06) / replicas
    scale = jnp.concatenate([scale] * TILES, axis=1)

    def near_body(g, carry):
        out_ref[g] = (near_ref[g] * scale).astype(BF)
        copy(g).start()
        return carry

    def far_body(i, carry):
        fetch(i).wait()
        g = groups - 1 - i
        out_ref[g] = (far_ref[i] * scale).astype(BF)
        copy(g).start()
        return carry

    lax.fori_loop(0, near, near_body, 0)
    lax.fori_loop(0, groups - near, far_body, 0)
    for g in range(groups):
        copy(g).wait()


def call(kernel, name, operands, out_shape, scratch=(), microseconds=1.0, aliases=()):
    specs, arrays = [], []
    for place, array in operands:
        specs.append(pl.BlockSpec(memory_space=place))
        arrays.append(pltpu.with_memory_space_constraint(array, place) if place is pltpu.HBM else array)
    shapes = out_shape if isinstance(out_shape, list) else [out_shape]
    outs = [
        pl.BlockSpec(memory_space=pltpu.HBM if shape.memory_space is pltpu.HBM else pltpu.VMEM)
        for shape in shapes
    ]
    return pl.pallas_call(
        kernel,
        in_specs=specs,
        out_specs=outs if isinstance(out_shape, list) else outs[0],
        out_shape=out_shape,
        scratch_shapes=list(scratch),
        input_output_aliases=dict(aliases),
        compiler_params=pltpu.CompilerParams(vmem_limit_bytes=VMEM_BYTES),
        cost_estimate=pl.CostEstimate(
            flops=0, bytes_accessed=int(microseconds * 3.0e6), transcendentals=0
        ),
        name=name,
    )(*arrays)


def per_device(momentum, kept, counts):
    _, rows, width = momentum.shape
    blocks = width // CH
    groups = width // WIDTH
    half = groups // 2
    replicas = lax.axis_size(REP)
    shards = lax.axis_size(FSDP)
    rep = lax.axis_index(REP).astype(jnp.int32).reshape(1)
    basis = pair_table()
    forward = jnp.asarray(split_weights(basis.T))
    inverse = jnp.asarray(split_weights(basis))
    hbm, vmem, smem = pltpu.HBM, pltpu.VMEM, pltpu.SMEM
    half_shape = (half, rows, LANES)
    flat = (half * rows, LANES)
    dma = pltpu.SemaphoreType.DMA
    turned = [vmem((2, LANES, LANES), jnp.float32)] * 3 + [vmem((2, TILES * rows, 2 * LANES), BF)]

    coeffs = vmem((2, TILES, rows, LANES), jnp.float32)

    numbers, live, other, x = call(
        pick_other_kernel,
        "pick_other",
        [
            (smem, rep),
            (hbm, momentum),
            (hbm, jnp.transpose(kept, (0, 2, 1))),
            (hbm, counts),
            (hbm, forward),
        ],
        [
            vmem((groups, rows, LANES), jnp.int32),
            vmem((groups, rows, LANES), jnp.float32),
            vmem(half_shape, jnp.float32),
            vmem((groups, rows, WIDTH), jnp.float32),
        ],
        [
            vmem((rows, KEEP, blocks), jnp.int32),
            vmem((rows, blocks), jnp.int32),
            vmem(forward.shape, BF),
            coeffs,
            dma((3,)),
            dma((groups,)),
        ],
        4.0,
    )
    mine = call(
        pick_mine_kernel,
        "pick_mine",
        [(smem, rep), (vmem, x), (vmem, numbers), (vmem, live), (vmem, forward)],
        vmem(half_shape, jnp.float32),
        [coeffs],
        2.0,
    )

    swap = [(i, i ^ 1) for i in range(replicas)]
    pieces = 1
    piece = vmem((flat[0] // pieces, LANES), jnp.float32)

    def add(name, left, right, after, out):
        counts = (len(left), len(right), len(out))
        return list(
            call(
                functools.partial(add_kernel, counts=counts),
                name,
                [(vmem, array) for array in left + right + after],
                out,
                microseconds=0.3,
            )
        )

    partner = lax.ppermute(other.reshape(flat), REP, swap)
    total = add("chip", [mine.reshape(flat)], [partner], [], [piece] * pieces)
    new_moment = None
    flips = []
    for part in range(2):
        pairs = []
        for y in range(replicas // 2):
            for core in range(2):
                there = y ^ 1 if part != core else (y + (1 if y % 2 else -1)) % (replicas // 2)
                pairs.append((2 * y + core, 2 * there + core))
        arrived = [lax.ppermute(some, REP, pairs) for some in total]
        earlier = [] if new_moment is None else [(hbm, new_moment)]
        new_moment, flipped, done = call(
            functools.partial(residue_kernel, part * half),
            f"residue_{part}",
            [
                (smem, rep),
                (vmem, x),
                (vmem, numbers),
                (vmem, mine),
                (vmem, other),
                (vmem, inverse),
                (vmem, total[0]),
            ]
            + earlier,
            [
                hbm(momentum.shape, jnp.float32),
                hbm((half, LANES, LANES), jnp.float32),
                vmem((8, LANES), jnp.float32),
            ],
            turned
            + [
                vmem((half, rows, WIDTH), jnp.float32),
                vmem((half, LANES, LANES), jnp.float32),
                dma((half,)),
                dma((half,)),
            ],
            2.5,
            {7: 0} if earlier else {},
        )
        flips.append(flipped)
        out = [vmem(flat, jnp.float32)] if part else [piece] * pieces
        total = add(f"sum_{part}", total, arrived, [done], out)
    (total,) = total
    own_energy, total = call(
        functools.partial(energy_kernel, replicas),
        "energy",
        [(vmem, total)],
        [vmem((2 * shards, 1, LANES), jnp.float32), vmem(flat, jnp.float32)],
        microseconds=0.5,
    )
    energies = lax.all_to_all(own_energy, ("core",) + FSDP, 0, 0, tiled=True)
    total_other = lax.ppermute(total, REP, swap)
    near = groups * 2 // 3
    far = groups - near
    near_raw, far_raw = call(
        raw_kernel,
        "raw",
        [
            (smem, rep),
            (hbm, flips[0]),
            (hbm, flips[1]),
            (vmem, total.reshape(half_shape)),
            (vmem, total_other.reshape(half_shape)),
            (hbm, inverse),
        ],
        [vmem((near, rows, WIDTH), jnp.float32), hbm((far, rows, WIDTH), jnp.float32)],
        turned
        + [
            vmem((far, rows, WIDTH), jnp.float32),
            vmem((groups, LANES, LANES), jnp.float32),
            vmem(inverse.shape, BF),
            dma((far,)),
            dma((3,)),
        ],
        5.0,
    )
    update = call(
        functools.partial(update_kernel, rows * width * shards, replicas),
        "update",
        [(vmem, near_raw), (hbm, far_raw), (vmem, energies)],
        hbm((rows, width), BF),
        [vmem((far, rows, WIDTH), jnp.float32), vmem((groups, rows, WIDTH), BF), dma((far,)), dma((groups,))],
        2.0,
    )
    return new_moment, update


def solution(mesh):
    cores = 2
    chips = mesh.shape["rep"] // cores
    lines = 4
    split = Mesh(
        mesh.devices.reshape(chips, cores, mesh.shape["fsdp"] // lines, lines), REP + FSDP
    )
    placed = (P(REP, FSDP, None), P(FSDP, None, None), P(None, FSDP, None))
    return jax.shard_map(
        per_device,
        mesh=split,
        in_specs=placed,
        out_specs=(P(REP, FSDP, None), P(FSDP, None)),
        check_vma=False,
    )
```

```python
import functools
import math

import jax
import jax.numpy as jnp
import ml_dtypes
import numpy as np
from jax import lax
from jax.experimental import pallas as pl
from jax.experimental.pallas import tpu as pltpu
from jax.sharding import Mesh, PartitionSpec as P

CH = 64
KEEP = 4
LANES = 128
PACK = 16
PAIR = LANES // CH
CELLS = LANES // KEEP
TILES = CELLS // PAIR
WIDTH = TILES * LANES
BF = jnp.bfloat16
REP = ("y", "core")
FSDP = ("z", "x")
VMEM_BYTES = 32 << 20
CHUNKS = 4


def pair_table():
    k, n = np.arange(CH)[:, None], np.arange(CH)[None, :]
    basis = np.cos(math.pi * (2 * n + 1) * k / (2 * CH)) * math.sqrt(2 / CH)
    basis[0] = math.sqrt(1 / CH)
    return np.kron(np.eye(PAIR), basis)


def split_weights(table):
    high = table.astype(ml_dtypes.bfloat16)
    low = (table - high.astype(np.float64)).astype(ml_dtypes.bfloat16)
    side = np.concatenate([high, low], axis=1)
    return np.concatenate([side, side], axis=0)


def halves(x):
    high = x.astype(BF)
    return high, (x - high.astype(jnp.float32)).astype(BF)


def apply_weights(tiles, weights):
    rows = tiles[0].shape[0]
    out = jnp.dot(jnp.concatenate(tiles, axis=0), weights, preferred_element_type=jnp.float32)
    out = out[:, :LANES] + out[:, LANES:]
    return [out[i * rows : (i + 1) * rows] for i in range(len(tiles))]


def lane_gather(x, index):
    return jnp.take_along_axis(x, index, axis=1, mode="promise_in_bounds")


def lane_ids(rows):
    return lax.broadcasted_iota(jnp.int32, (rows, LANES), 1)


def spread(value, group, rows):
    start = group * CELLS
    base = start // LANES * LANES
    part = value[:, base : base + LANES]
    if part.shape[1] < LANES:
        part = jnp.pad(part, ((0, 0), (0, LANES - part.shape[1])))
    return lane_gather(part, start - base + lane_ids(rows) % CELLS)


def flip(x):
    fill = LANES - x.shape[0]
    return jnp.concatenate([x, x[:fill]], axis=0).T if fill else x.T


def columns(group):
    return pl.ds(pl.multiple_of(group * WIDTH, WIDTH), WIDTH)


def choose_groups(x_ref, number_ref, live_ref, w_ref, coeff_ref, out_ref, first_group):
    count, rows, _ = out_ref.shape
    lanes = lane_ids(8)
    block_start = lanes % PAIR * CH
    tile_of = lanes % CELLS // PAIR

    def transform(i, buffer, tiles):
        g = first_group + i
        parts = [
            jnp.concatenate(halves(x_ref[g, :, t * LANES : (t + 1) * LANES]), axis=1) for t in tiles
        ]
        for t, coeffs in zip(tiles, apply_weights(parts, w_ref[...])):
            coeff_ref[buffer, t] = coeffs

    def choose(i, buffer, first):
        here = slice(first, first + 8)
        index = number_ref[first_group + i, here] + block_start
        picked = jnp.zeros((8, LANES), jnp.float32)
        for t in range(TILES):
            picked = jnp.where(tile_of == t, lane_gather(coeff_ref[buffer, t, here], index), picked)
        out_ref[i, here] = jnp.where(live_ref[first_group + i, here] > 0.0, picked, 0.0)

    transform(0, 0, range(TILES))
    for i in range(count - 1):
        for j in range(CHUNKS):
            transform(i + 1, (i + 1) % 2, span(TILES, j))
            for part in span(rows // 8, j):
                choose(i, i % 2, 8 * part)
    for part in range(rows // 8):
        choose(count - 1, (count - 1) % 2, 8 * part)


def pick_other_kernel(
    rep_ref, x_hbm, kept_hbm, cnt_hbm, w_hbm, number_ref, live_ref, other_ref, x_ref,
    kept_ref, cnt_ref, w_ref, coeff_ref, small_sem, x_sem,
):
    groups, rows, _ = x_ref.shape
    half = groups // 2
    core = rep_ref[0] % 2
    theirs, ours = (1 - core) * half, core * half
    small = [
        pltpu.make_async_copy(w_hbm, w_ref, small_sem.at[0]),
        pltpu.make_async_copy(kept_hbm, kept_ref, small_sem.at[1]),
        pltpu.make_async_copy(cnt_hbm.at[rep_ref[0]], cnt_ref, small_sem.at[2]),
    ]
    for copy in small:
        copy.start()

    def x_copy(first, i):
        g = first + i
        return pltpu.make_async_copy(x_hbm.at[0, :, columns(g)], x_ref.at[g], x_sem.at[g])

    for i in range(half):
        x_copy(theirs, i).start()
    for copy in small:
        copy.wait()
    for i in range(half):
        x_copy(theirs, i).wait()
    for i in range(half):
        x_copy(ours, i).start()

    slot = lane_ids(rows) // CELLS
    counts = cnt_ref[...]
    numbers = [kept_ref[:, s, :] for s in range(KEEP)]
    for g in range(groups):
        chosen = spread(numbers[0], g, rows)
        for s in range(1, KEEP):
            chosen = jnp.where(slot == s, spread(numbers[s], g, rows), chosen)
        number_ref[g] = chosen
        live_ref[g] = jnp.where(slot < spread(counts, g, rows), 1.0, 0.0)

    choose_groups(x_ref, number_ref, live_ref, w_ref, coeff_ref, other_ref, theirs)
    for i in range(half):
        x_copy(ours, i).wait()


def pick_mine_kernel(rep_ref, x_ref, number_ref, live_ref, w_ref, mine_ref, coeff_ref):
    first = rep_ref[0] % 2 * mine_ref.shape[0]
    choose_groups(x_ref, number_ref, live_ref, w_ref, coeff_ref, mine_ref, first)


def span(count, j):
    return range(count * j // CHUNKS, count * (j + 1) // CHUNKS)


def two_by_two(step, count):
    def body(i, carry):
        step(2 * i, 0)
        step(2 * i + 1, 1)
        return carry

    lax.fori_loop(0, count // 2, body, 0)
    if count % 2:
        step(count - 1, (count - 1) % 2)


def decode(groups, numbers_of, values_of, w_ref, number_ref, high_ref, low_ref, dense_ref, store, unroll):
    rows = dense_ref.shape[1] // TILES
    ids = lax.broadcasted_iota(jnp.int32, (PACK, LANES), 0).astype(jnp.float32)
    ids = [(ids + first).astype(BF) for first in range(0, CH, PACK)]
    zero = jnp.zeros((PACK, LANES), BF)

    def turn(g, buffer):
        number_ref[buffer] = numbers_of(g)
        values = flip(values_of(g))
        high = values.astype(BF).astype(jnp.float32)
        high_ref[buffer] = high
        low_ref[buffer] = values - high

    def row(ref, buffer, s, cell):
        at = s * CELLS + cell
        return jnp.broadcast_to(ref[buffer, at : at + 1, :], (PACK, LANES)).astype(BF)

    def fill(buffer, tiles):
        for t in tiles:
            highs, lows = [], []
            for cell in range(t * PAIR, (t + 1) * PAIR):
                kept = [row(number_ref, buffer, s, cell) for s in range(KEEP)]
                cell_high = [row(high_ref, buffer, s, cell) for s in range(KEEP)]
                cell_low = [row(low_ref, buffer, s, cell) for s in range(KEEP)]
                for some in ids:
                    dense_high, dense_low = zero, zero
                    for s in range(KEEP):
                        hit = kept[s] == some
                        dense_high = jnp.where(hit, cell_high[s], dense_high)
                        dense_low = jnp.where(hit, cell_low[s], dense_low)
                    highs.append(dense_high)
                    lows.append(dense_low)
            here = slice(t * rows, (t + 1) * rows)
            dense_ref[buffer, here, :LANES] = jnp.concatenate(highs, axis=0).T[:rows]
            dense_ref[buffer, here, LANES:] = jnp.concatenate(lows, axis=0).T[:rows]

    def product(g, buffer, tiles):
        parts = [dense_ref[buffer, t * rows : (t + 1) * rows] for t in tiles]
        for t, part in zip(tiles, apply_weights(parts, w_ref[...])):
            store(g, t, part)

    def step(g, buffer):
        turn(g + 1, 1 - buffer)
        for j in range(CHUNKS):
            product(g, buffer, span(TILES, j))
            fill(1 - buffer, span(TILES, j))
        store(g, None, None)

    turn(0, 0)
    fill(0, range(TILES))
    if unroll:
        for g in range(groups - 1):
            step(g, g % 2)
    else:
        two_by_two(step, groups - 1)
    product(groups - 1, (groups - 1) % 2, range(TILES))
    store(groups - 1, None, None)


def side(rep_ref, mine_ref, other_ref, g):
    half = mine_ref.shape[0]
    return jnp.where(g // half == rep_ref[0] % 2, mine_ref[g % half], other_ref[g % half])


def residue_kernel(
    first, rep_ref, x_ref, chosen_ref, mine_ref, other_ref, w_ref, after_ref, *refs
):
    (
        out_hbm, flip_hbm, done_ref, number_ref, high_ref, low_ref, dense_ref, out_ref, flip_ref, sem, flip_sem,
    ) = refs[-11:]
    count = out_ref.shape[0]
    done_ref[...] = jnp.zeros(done_ref.shape, jnp.float32)

    def copy(i):
        return pltpu.make_async_copy(out_ref.at[i], out_hbm.at[0, :, columns(first + i)], sem.at[i])

    def flip_copy(i):
        return pltpu.make_async_copy(flip_ref.at[i], flip_hbm.at[first + i], flip_sem.at[i])

    def numbers_of(i):
        turned = flip(chosen_ref[first + i].astype(jnp.float32))
        flip_ref[i] = turned
        flip_copy(i).start()
        return turned

    def store(i, t, part):
        if t is None:
            copy(i).start()
        else:
            here = slice(t * LANES, (t + 1) * LANES)
            out_ref[i, :, here] = x_ref[first + i, :, here] - part

    decode(
        count, numbers_of, lambda i: side(rep_ref, mine_ref, other_ref, first + i), w_ref,
        number_ref, high_ref, low_ref, dense_ref, store, False,
    )
    for i in range(count):
        copy(i).wait()
        flip_copy(i).wait()


def add_kernel(*refs, counts):
    refs = list(refs)
    left, right = [[refs.pop(0) for _ in range(count)] for count in counts[:2]]
    outs = refs[len(refs) - counts[2] :]
    left, right = [jnp.concatenate([ref[...] for ref in part], axis=0) for part in (left, right)]
    total = left + right
    at = 0
    for out in outs:
        out[...] = total[at : at + out.shape[0]]
        at += out.shape[0]


def energy_kernel(replicas, total_ref, out_ref, total_out_ref, saved_ref):
    total = total_ref[...]
    total_out_ref[...] = total
    saved_ref[...] = total
    square = jnp.square(total / replicas)
    energy = jnp.sum(jnp.sum(square, axis=0, keepdims=True), axis=1, keepdims=True)
    out_ref[...] = jnp.broadcast_to(energy[None], out_ref.shape)


def raw_kernel(
    rep_ref, flip_hbm, mine_hbm, other_hbm, w_hbm, near_ref, value_out_ref, flip_out_ref, w_ref,
    number_ref, high_ref, low_ref, dense_ref, flip_ref, mine_ref, other_ref, sem,
):
    near, far = near_ref.shape[0], flip_out_ref.shape[0]
    fetches = [
        pltpu.make_async_copy(flip_hbm.at[:near], flip_ref, sem.at[0]),
        pltpu.make_async_copy(flip_hbm.at[near:], flip_out_ref, sem.at[1]),
        pltpu.make_async_copy(mine_hbm, mine_ref, sem.at[2]),
        pltpu.make_async_copy(other_hbm, other_ref, sem.at[3]),
        pltpu.make_async_copy(w_hbm, w_ref, sem.at[4]),
    ]
    for fetch in fetches:
        fetch.start()
    for fetch in fetches:
        fetch.wait()

    def store(g, t, part):
        if t is not None:
            near_ref[g, :, t * LANES : (t + 1) * LANES] = part

    decode(
        near, lambda g: flip_ref[g], lambda g: side(rep_ref, mine_ref, other_ref, g), w_ref,
        number_ref, high_ref, low_ref, dense_ref, store, True,
    )
    for i in range(far):
        value_out_ref[i] = side(rep_ref, mine_ref, other_ref, near + i)


def update_kernel(
    entries, replicas, near_ref, value_ref, flip_ref, w_ref, energy_ref, out_hbm,
    number_ref, high_ref, low_ref, dense_ref, out_ref, sem,
):
    groups = out_ref.shape[0]
    near = near_ref.shape[0]
    energy = jnp.sum(energy_ref[:, 0, :], axis=0, keepdims=True)
    scale = lax.rsqrt(energy / entries + 1e-06) / replicas
    wide = jnp.concatenate([scale] * TILES, axis=1)

    def copy(g):
        return pltpu.make_async_copy(out_ref.at[g], out_hbm.at[:, columns(g)], sem.at[g])

    for g in range(near):
        out_ref[g] = (near_ref[g] * wide).astype(BF)
        copy(g).start()

    def store(i, t, part):
        if t is None:
            copy(near + i).start()
        else:
            out_ref[near + i, :, t * LANES : (t + 1) * LANES] = part.astype(BF)

    decode(
        groups - near, lambda i: flip_ref[i], lambda i: value_ref[i] * scale, w_ref,
        number_ref, high_ref, low_ref, dense_ref, store, True,
    )
    for g in range(groups):
        copy(g).wait()


def call(kernel, name, operands, out_shape, scratch=(), microseconds=1.0, aliases=(), blocked=False):
    specs, arrays = [], []
    for place, array in operands:
        specs.append(pl.BlockSpec(memory_space=place))
        arrays.append(pltpu.with_memory_space_constraint(array, place) if place is pltpu.HBM else array)
    shapes = out_shape if isinstance(out_shape, list) else [out_shape]
    outs = [
        pl.BlockSpec(memory_space=pltpu.HBM if shape.memory_space is pltpu.HBM and not blocked else pltpu.VMEM)
        for shape in shapes
    ]
    return pl.pallas_call(
        kernel,
        in_specs=specs,
        out_specs=outs if isinstance(out_shape, list) else outs[0],
        out_shape=out_shape,
        scratch_shapes=list(scratch),
        input_output_aliases=dict(aliases),
        compiler_params=pltpu.CompilerParams(vmem_limit_bytes=VMEM_BYTES),
        cost_estimate=pl.CostEstimate(
            flops=0, bytes_accessed=int(microseconds * 3.0e6), transcendentals=0
        ),
        name=name,
    )(*arrays)


def per_device(momentum, kept, counts):
    _, rows, width = momentum.shape
    blocks = width // CH
    groups = width // WIDTH
    half = groups // 2
    replicas = lax.axis_size(REP)
    shards = lax.axis_size(FSDP)
    rep = lax.axis_index(REP).astype(jnp.int32).reshape(1)
    basis = pair_table()
    forward = jnp.asarray(split_weights(basis.T))
    inverse = jnp.asarray(split_weights(basis))
    hbm, vmem, smem = pltpu.HBM, pltpu.VMEM, pltpu.SMEM
    half_shape = (half, rows, LANES)
    flat = (half * rows, LANES)
    dma = pltpu.SemaphoreType.DMA
    turned = [vmem((2, LANES, LANES), jnp.float32)] * 3 + [vmem((2, TILES * rows, 2 * LANES), BF)]

    coeffs = vmem((2, TILES, rows, LANES), jnp.float32)

    numbers, live, other, x = call(
        pick_other_kernel,
        "pick_other",
        [
            (smem, rep),
            (hbm, momentum),
            (hbm, jnp.transpose(kept, (0, 2, 1))),
            (hbm, counts),
            (hbm, forward),
        ],
        [
            vmem((groups, rows, LANES), jnp.int32),
            vmem((groups, rows, LANES), jnp.float32),
            vmem(half_shape, jnp.float32),
            vmem((groups, rows, WIDTH), jnp.float32),
        ],
        [
            vmem((rows, KEEP, blocks), jnp.int32),
            vmem((rows, blocks), jnp.int32),
            vmem(forward.shape, BF),
            coeffs,
            dma((3,)),
            dma((groups,)),
        ],
        4.0,
    )
    mine = call(
        pick_mine_kernel,
        "pick_mine",
        [(smem, rep), (vmem, x), (vmem, numbers), (vmem, live), (vmem, forward)],
        vmem(half_shape, jnp.float32),
        [coeffs],
        2.0,
    )

    swap = [(i, i ^ 1) for i in range(replicas)]
    pieces = 1
    piece = vmem((flat[0] // pieces, LANES), jnp.float32)

    def add(name, left, right, after, out):
        counts = (len(left), len(right), len(out))
        return list(
            call(
                functools.partial(add_kernel, counts=counts),
                name,
                [(vmem, array) for array in left + right + after],
                out,
                microseconds=0.3,
            )
        )

    partner = lax.ppermute(other.reshape(flat), REP, swap)
    total = add("chip", [mine.reshape(flat)], [partner], [], [piece] * pieces)
    new_moment = None
    for part in range(2):
        pairs = []
        for y in range(replicas // 2):
            for core in range(2):
                there = y ^ 1 if part != core else (y + (1 if y % 2 else -1)) % (replicas // 2)
                pairs.append((2 * y + core, 2 * there + core))
        arrived = [lax.ppermute(some, REP, pairs) for some in total]
        earlier = [] if new_moment is None else [(hbm, new_moment), (hbm, flips)]
        new_moment, flips, done = call(
            functools.partial(residue_kernel, part * half),
            f"residue_{part}",
            [
                (smem, rep),
                (vmem, x),
                (vmem, numbers),
                (vmem, mine),
                (vmem, other),
                (vmem, inverse),
                (vmem, total[0]),
            ]
            + earlier,
            [
                hbm(momentum.shape, jnp.float32),
                hbm((groups, LANES, LANES), jnp.float32),
                vmem((8, LANES), jnp.float32),
            ],
            turned
            + [
                vmem((half, rows, WIDTH), jnp.float32),
                vmem((half, LANES, LANES), jnp.float32),
                dma((half,)),
                dma((half,)),
            ],
            2.5,
            {7: 0, 8: 1} if earlier else {},
        )
        out = [vmem(flat, jnp.float32)] if part else [piece] * pieces
        total = add(f"sum_{part}", total, arrived, [done], out)
    (total,) = total
    own_energy, total, saved = call(
        functools.partial(energy_kernel, replicas),
        "energy",
        [(vmem, total)],
        [vmem((2 * shards, 1, LANES), jnp.float32), vmem(flat, jnp.float32), hbm(flat, jnp.float32)],
        microseconds=0.5,
        blocked=True,
    )
    energies = lax.all_to_all(own_energy, ("core",) + FSDP, 0, 0, tiled=True)
    total_other = lax.ppermute(total, REP, swap)
    near = groups * 2 // 3
    far = groups - near
    raw, values, turns, weights = call(
        raw_kernel,
        "raw",
        [
            (smem, rep),
            (hbm, flips),
            (hbm, saved.reshape(half_shape)),
            (hbm, total_other.reshape(half_shape)),
            (hbm, inverse),
        ],
        [
            vmem((near, rows, WIDTH), jnp.float32),
            vmem((far, rows, LANES), jnp.float32),
            vmem((far, LANES, LANES), jnp.float32),
            vmem(inverse.shape, BF),
        ],
        turned
        + [
            vmem((near, LANES, LANES), jnp.float32),
            vmem(half_shape, jnp.float32),
            vmem(half_shape, jnp.float32),
            dma((5,)),
        ],
        5.0,
    )
    update = call(
        functools.partial(update_kernel, rows * width * shards, replicas),
        "update",
        [(vmem, raw), (vmem, values), (vmem, turns), (vmem, weights), (vmem, energies)],
        hbm((rows, width), BF),
        turned + [vmem((groups, rows, WIDTH), BF), dma((groups,))],
        2.0,
    )
    return new_moment, update


def solution(mesh):
    cores = 2
    chips = mesh.shape["rep"] // cores
    lines = 4
    split = Mesh(
        mesh.devices.reshape(chips, cores, mesh.shape["fsdp"] // lines, lines), REP + FSDP
    )
    placed = (P(REP, FSDP, None), P(FSDP, None, None), P(None, FSDP, None))
    return jax.shard_map(
        per_device,
        mesh=split,
        in_specs=placed,
        out_specs=(P(REP, FSDP, None), P(FSDP, None)),
        check_vma=False,
    )
```

```python
import functools
import math

import jax
import jax.numpy as jnp
import ml_dtypes
import numpy as np
from jax import lax
from jax.experimental import pallas as pl
from jax.experimental.pallas import tpu as pltpu
from jax.sharding import Mesh, PartitionSpec as P

CH = 64
KEEP = 4
LANES = 128
PACK = 16
PAIR = LANES // CH
CELLS = LANES // KEEP
TILES = CELLS // PAIR
WIDTH = TILES * LANES
BF = jnp.bfloat16
REP = ("y", "core")
FSDP = ("z", "x")
VMEM_BYTES = 32 << 20
CHUNKS = 4


def pair_table():
    k, n = np.arange(CH)[:, None], np.arange(CH)[None, :]
    basis = np.cos(math.pi * (2 * n + 1) * k / (2 * CH)) * math.sqrt(2 / CH)
    basis[0] = math.sqrt(1 / CH)
    return np.kron(np.eye(PAIR), basis)


def split_weights(table):
    high = table.astype(ml_dtypes.bfloat16)
    low = (table - high.astype(np.float64)).astype(ml_dtypes.bfloat16)
    side = np.concatenate([high, low], axis=1)
    return np.concatenate([side, side], axis=0)


def halves(x):
    high = x.astype(BF)
    return high, (x - high.astype(jnp.float32)).astype(BF)


def apply_weights(tiles, weights):
    rows = tiles[0].shape[0]
    out = jnp.dot(jnp.concatenate(tiles, axis=0), weights, preferred_element_type=jnp.float32)
    out = out[:, :LANES] + out[:, LANES:]
    return [out[i * rows : (i + 1) * rows] for i in range(len(tiles))]


def lane_gather(x, index):
    return jnp.take_along_axis(x, index, axis=1, mode="promise_in_bounds")


def lane_ids(rows):
    return lax.broadcasted_iota(jnp.int32, (rows, LANES), 1)


def spread(value, group, rows):
    start = group * CELLS
    base = start // LANES * LANES
    part = value[:, base : base + LANES]
    if part.shape[1] < LANES:
        part = jnp.pad(part, ((0, 0), (0, LANES - part.shape[1])))
    return lane_gather(part, start - base + lane_ids(rows) % CELLS)


def flip(x):
    fill = LANES - x.shape[0]
    return jnp.concatenate([x, x[:fill]], axis=0).T if fill else x.T


def columns(group):
    return pl.ds(pl.multiple_of(group * WIDTH, WIDTH), WIDTH)


def choose_groups(x_ref, number_ref, live_ref, w_ref, coeff_ref, out_ref, first_group):
    count, rows, _ = out_ref.shape
    lanes = lane_ids(8)
    block_start = lanes % PAIR * CH
    tile_of = lanes % CELLS // PAIR

    def transform(i, buffer, tiles):
        g = first_group + i
        parts = [
            jnp.concatenate(halves(x_ref[g, :, t * LANES : (t + 1) * LANES]), axis=1) for t in tiles
        ]
        for t, coeffs in zip(tiles, apply_weights(parts, w_ref[...])):
            coeff_ref[buffer, t] = coeffs

    def choose(i, buffer, first):
        here = slice(first, first + 8)
        index = number_ref[first_group + i, here] + block_start
        picked = jnp.zeros((8, LANES), jnp.float32)
        for t in range(TILES):
            picked = jnp.where(tile_of == t, lane_gather(coeff_ref[buffer, t, here], index), picked)
        out_ref[i, here] = jnp.where(live_ref[first_group + i, here] > 0.0, picked, 0.0)

    transform(0, 0, range(TILES))
    for i in range(count - 1):
        for j in range(CHUNKS):
            transform(i + 1, (i + 1) % 2, span(TILES, j))
            for part in span(rows // 8, j):
                choose(i, i % 2, 8 * part)
    for part in range(rows // 8):
        choose(count - 1, (count - 1) % 2, 8 * part)


def pick_other_kernel(
    rep_ref, x_hbm, kept_hbm, cnt_hbm, w_hbm, number_ref, live_ref, other_ref, x_ref,
    kept_ref, cnt_ref, w_ref, coeff_ref, small_sem, x_sem,
):
    groups, rows, _ = x_ref.shape
    half = groups // 2
    core = rep_ref[0] % 2
    theirs, ours = (1 - core) * half, core * half
    small = [
        pltpu.make_async_copy(w_hbm, w_ref, small_sem.at[0]),
        pltpu.make_async_copy(kept_hbm, kept_ref, small_sem.at[1]),
        pltpu.make_async_copy(cnt_hbm.at[rep_ref[0]], cnt_ref, small_sem.at[2]),
    ]
    for copy in small:
        copy.start()

    def x_copy(first, i):
        g = first + i
        return pltpu.make_async_copy(x_hbm.at[0, :, columns(g)], x_ref.at[g], x_sem.at[g])

    for i in range(half):
        x_copy(theirs, i).start()
    for copy in small:
        copy.wait()
    for i in range(half):
        x_copy(theirs, i).wait()
    for i in range(half):
        x_copy(ours, i).start()

    slot = lane_ids(rows) // CELLS
    counts = cnt_ref[...]
    numbers = [kept_ref[:, s, :] for s in range(KEEP)]
    for g in range(groups):
        chosen = spread(numbers[0], g, rows)
        for s in range(1, KEEP):
            chosen = jnp.where(slot == s, spread(numbers[s], g, rows), chosen)
        number_ref[g] = chosen
        live_ref[g] = jnp.where(slot < spread(counts, g, rows), 1.0, 0.0)

    choose_groups(x_ref, number_ref, live_ref, w_ref, coeff_ref, other_ref, theirs)
    for i in range(half):
        x_copy(ours, i).wait()


def pick_mine_kernel(rep_ref, x_ref, number_ref, live_ref, w_ref, mine_ref, coeff_ref):
    first = rep_ref[0] % 2 * mine_ref.shape[0]
    choose_groups(x_ref, number_ref, live_ref, w_ref, coeff_ref, mine_ref, first)


def span(count, j):
    return range(count * j // CHUNKS, count * (j + 1) // CHUNKS)


def two_by_two(step, count):
    def body(i, carry):
        step(2 * i, 0)
        step(2 * i + 1, 1)
        return carry

    lax.fori_loop(0, count // 2, body, 0)
    if count % 2:
        step(count - 1, (count - 1) % 2)


def decode(groups, numbers_of, values_of, w_ref, number_ref, high_ref, low_ref, dense_ref, store, unroll):
    rows = dense_ref.shape[1] // TILES
    ids = lax.broadcasted_iota(jnp.int32, (PACK, LANES), 0).astype(jnp.float32)
    ids = [(ids + first).astype(BF) for first in range(0, CH, PACK)]
    zero = jnp.zeros((PACK, LANES), BF)

    def turn(g, buffer):
        number_ref[buffer] = numbers_of(g)
        values = flip(values_of(g))
        high = values.astype(BF).astype(jnp.float32)
        high_ref[buffer] = high
        low_ref[buffer] = values - high

    def row(ref, buffer, s, cell):
        at = s * CELLS + cell
        return jnp.broadcast_to(ref[buffer, at : at + 1, :], (PACK, LANES)).astype(BF)

    def fill(buffer, tiles):
        for t in tiles:
            highs, lows = [], []
            for cell in range(t * PAIR, (t + 1) * PAIR):
                kept = [row(number_ref, buffer, s, cell) for s in range(KEEP)]
                cell_high = [row(high_ref, buffer, s, cell) for s in range(KEEP)]
                cell_low = [row(low_ref, buffer, s, cell) for s in range(KEEP)]
                for some in ids:
                    dense_high, dense_low = zero, zero
                    for s in range(KEEP):
                        hit = kept[s] == some
                        dense_high = jnp.where(hit, cell_high[s], dense_high)
                        dense_low = jnp.where(hit, cell_low[s], dense_low)
                    highs.append(dense_high)
                    lows.append(dense_low)
            here = slice(t * rows, (t + 1) * rows)
            dense_ref[buffer, here, :LANES] = jnp.concatenate(highs, axis=0).T[:rows]
            dense_ref[buffer, here, LANES:] = jnp.concatenate(lows, axis=0).T[:rows]

    def product(g, buffer, tiles):
        parts = [dense_ref[buffer, t * rows : (t + 1) * rows] for t in tiles]
        for t, part in zip(tiles, apply_weights(parts, w_ref[...])):
            store(g, t, part)

    def step(g, buffer):
        turn(g + 1, 1 - buffer)
        for j in range(CHUNKS):
            product(g, buffer, span(TILES, j))
            fill(1 - buffer, span(TILES, j))
        store(g, None, None)

    turn(0, 0)
    fill(0, range(TILES))
    if unroll:
        for g in range(groups - 1):
            step(g, g % 2)
    else:
        two_by_two(step, groups - 1)
    product(groups - 1, (groups - 1) % 2, range(TILES))
    store(groups - 1, None, None)


def side(rep_ref, mine_ref, other_ref, g):
    half = mine_ref.shape[0]
    return jnp.where(g // half == rep_ref[0] % 2, mine_ref[g % half], other_ref[g % half])


def residue_kernel(
    first, rep_ref, x_ref, chosen_ref, mine_ref, other_ref, w_ref, after_ref, *refs
):
    (
        out_hbm, flip_hbm, done_ref, number_ref, high_ref, low_ref, dense_ref, out_ref, flip_ref, sem, flip_sem,
    ) = refs[-11:]
    count = out_ref.shape[0]
    done_ref[...] = jnp.zeros(done_ref.shape, jnp.float32)

    def copy(i):
        return pltpu.make_async_copy(out_ref.at[i], out_hbm.at[0, :, columns(first + i)], sem.at[i])

    def flip_copy(i):
        return pltpu.make_async_copy(flip_ref.at[i], flip_hbm.at[first + i], flip_sem.at[i])

    def numbers_of(i):
        turned = flip(chosen_ref[first + i].astype(jnp.float32))
        flip_ref[i] = turned
        flip_copy(i).start()
        return turned

    def store(i, t, part):
        if t is None:
            copy(i).start()
        else:
            here = slice(t * LANES, (t + 1) * LANES)
            out_ref[i, :, here] = x_ref[first + i, :, here] - part

    decode(
        count, numbers_of, lambda i: side(rep_ref, mine_ref, other_ref, first + i), w_ref,
        number_ref, high_ref, low_ref, dense_ref, store, False,
    )
    for i in range(count):
        copy(i).wait()
        flip_copy(i).wait()


def add_kernel(*refs, counts):
    refs = list(refs)
    left, right = [[refs.pop(0) for _ in range(count)] for count in counts[:2]]
    outs = refs[len(refs) - counts[2] :]
    left, right = [jnp.concatenate([ref[...] for ref in part], axis=0) for part in (left, right)]
    total = left + right
    at = 0
    for out in outs:
        out[...] = total[at : at + out.shape[0]]
        at += out.shape[0]


def energy_kernel(replicas, total_ref, out_ref, total_out_ref, saved_ref):
    total = total_ref[...]
    total_out_ref[...] = total
    saved_ref[...] = total
    square = jnp.square(total / replicas)
    energy = jnp.sum(jnp.sum(square, axis=0, keepdims=True), axis=1, keepdims=True)
    out_ref[...] = jnp.broadcast_to(energy[None], out_ref.shape)


def raw_kernel(
    rep_ref, flip_hbm, mine_hbm, other_hbm, w_hbm, near_ref, value_out_ref, flip_out_ref, w_ref,
    number_ref, high_ref, low_ref, dense_ref, flip_ref, mine_ref, other_ref, sem,
):
    near, far = near_ref.shape[0], flip_out_ref.shape[0]
    fetches = [
        pltpu.make_async_copy(flip_hbm.at[:near], flip_ref, sem.at[0]),
        pltpu.make_async_copy(flip_hbm.at[near:], flip_out_ref, sem.at[1]),
        pltpu.make_async_copy(mine_hbm, mine_ref, sem.at[2]),
        pltpu.make_async_copy(other_hbm, other_ref, sem.at[3]),
        pltpu.make_async_copy(w_hbm, w_ref, sem.at[4]),
    ]
    for fetch in fetches:
        fetch.start()
    for fetch in fetches:
        fetch.wait()

    def store(g, t, part):
        if t is not None:
            near_ref[g, :, t * LANES : (t + 1) * LANES] = part

    decode(
        near, lambda g: flip_ref[g], lambda g: side(rep_ref, mine_ref, other_ref, g), w_ref,
        number_ref, high_ref, low_ref, dense_ref, store, True,
    )
    for i in range(far):
        value_out_ref[i] = side(rep_ref, mine_ref, other_ref, near + i)


def update_kernel(
    entries, replicas, near_ref, value_ref, flip_ref, w_ref, energy_ref, out_hbm,
    number_ref, high_ref, low_ref, dense_ref, out_ref, sem,
):
    groups = out_ref.shape[0]
    near = near_ref.shape[0]
    energy = jnp.sum(energy_ref[:, 0, :], axis=0, keepdims=True)
    scale = lax.rsqrt(energy / entries + 1e-06) / replicas
    wide = jnp.concatenate([scale] * TILES, axis=1)

    def copy(g):
        return pltpu.make_async_copy(out_ref.at[g], out_hbm.at[:, columns(g)], sem.at[g])

    early = near // 2
    for g in range(early):
        out_ref[g] = (near_ref[g] * wide).astype(BF)
        copy(g).start()

    def store(i, t, part):
        if t is None:
            for g in range(early, near) if i == 0 else ():
                copy(g).start()
            copy(near + i).start()
        else:
            here = slice(t * LANES, (t + 1) * LANES)
            for g in range(early, near) if i == 0 else ():
                out_ref[g, :, here] = (near_ref[g, :, here] * scale).astype(BF)
            out_ref[near + i, :, here] = part.astype(BF)

    decode(
        groups - near, lambda i: flip_ref[i], lambda i: value_ref[i] * scale, w_ref,
        number_ref, high_ref, low_ref, dense_ref, store, True,
    )
    for g in range(groups):
        copy(g).wait()


def call(kernel, name, operands, out_shape, scratch=(), microseconds=1.0, aliases=(), blocked=False):
    specs, arrays = [], []
    for place, array in operands:
        specs.append(pl.BlockSpec(memory_space=place))
        arrays.append(pltpu.with_memory_space_constraint(array, place) if place is pltpu.HBM else array)
    shapes = out_shape if isinstance(out_shape, list) else [out_shape]
    outs = [
        pl.BlockSpec(memory_space=pltpu.HBM if shape.memory_space is pltpu.HBM and not blocked else pltpu.VMEM)
        for shape in shapes
    ]
    return pl.pallas_call(
        kernel,
        in_specs=specs,
        out_specs=outs if isinstance(out_shape, list) else outs[0],
        out_shape=out_shape,
        scratch_shapes=list(scratch),
        input_output_aliases=dict(aliases),
        compiler_params=pltpu.CompilerParams(vmem_limit_bytes=VMEM_BYTES),
        cost_estimate=pl.CostEstimate(
            flops=0, bytes_accessed=int(microseconds * 3.0e6), transcendentals=0
        ),
        name=name,
    )(*arrays)


def per_device(momentum, kept, counts):
    _, rows, width = momentum.shape
    blocks = width // CH
    groups = width // WIDTH
    half = groups // 2
    replicas = lax.axis_size(REP)
    shards = lax.axis_size(FSDP)
    rep = lax.axis_index(REP).astype(jnp.int32).reshape(1)
    basis = pair_table()
    forward = jnp.asarray(split_weights(basis.T))
    inverse = jnp.asarray(split_weights(basis))
    hbm, vmem, smem = pltpu.HBM, pltpu.VMEM, pltpu.SMEM
    half_shape = (half, rows, LANES)
    flat = (half * rows, LANES)
    dma = pltpu.SemaphoreType.DMA
    turned = [vmem((2, LANES, LANES), jnp.float32)] * 3 + [vmem((2, TILES * rows, 2 * LANES), BF)]

    coeffs = vmem((2, TILES, rows, LANES), jnp.float32)

    numbers, live, other, x = call(
        pick_other_kernel,
        "pick_other",
        [
            (smem, rep),
            (hbm, momentum),
            (hbm, jnp.transpose(kept, (0, 2, 1))),
            (hbm, counts),
            (hbm, forward),
        ],
        [
            vmem((groups, rows, LANES), jnp.int32),
            vmem((groups, rows, LANES), jnp.float32),
            vmem(half_shape, jnp.float32),
            vmem((groups, rows, WIDTH), jnp.float32),
        ],
        [
            vmem((rows, KEEP, blocks), jnp.int32),
            vmem((rows, blocks), jnp.int32),
            vmem(forward.shape, BF),
            coeffs,
            dma((3,)),
            dma((groups,)),
        ],
        4.0,
    )
    mine = call(
        pick_mine_kernel,
        "pick_mine",
        [(smem, rep), (vmem, x), (vmem, numbers), (vmem, live), (vmem, forward)],
        vmem(half_shape, jnp.float32),
        [coeffs],
        2.0,
    )

    swap = [(i, i ^ 1) for i in range(replicas)]
    pieces = 1
    piece = vmem((flat[0] // pieces, LANES), jnp.float32)

    def add(name, left, right, after, out):
        counts = (len(left), len(right), len(out))
        return list(
            call(
                functools.partial(add_kernel, counts=counts),
                name,
                [(vmem, array) for array in left + right + after],
                out,
                microseconds=0.3,
            )
        )

    partner = lax.ppermute(other.reshape(flat), REP, swap)
    total = add("chip", [mine.reshape(flat)], [partner], [], [piece] * pieces)
    new_moment = None
    for part in range(2):
        pairs = []
        for y in range(replicas // 2):
            for core in range(2):
                there = y ^ 1 if part != core else (y + (1 if y % 2 else -1)) % (replicas // 2)
                pairs.append((2 * y + core, 2 * there + core))
        arrived = [lax.ppermute(some, REP, pairs) for some in total]
        earlier = [] if new_moment is None else [(hbm, new_moment), (hbm, flips)]
        new_moment, flips, done = call(
            functools.partial(residue_kernel, part * half),
            f"residue_{part}",
            [
                (smem, rep),
                (vmem, x),
                (vmem, numbers),
                (vmem, mine),
                (vmem, other),
                (vmem, inverse),
                (vmem, total[0]),
            ]
            + earlier,
            [
                hbm(momentum.shape, jnp.float32),
                hbm((groups, LANES, LANES), jnp.float32),
                vmem((8, LANES), jnp.float32),
            ],
            turned
            + [
                vmem((half, rows, WIDTH), jnp.float32),
                vmem((half, LANES, LANES), jnp.float32),
                dma((half,)),
                dma((half,)),
            ],
            2.5,
            {7: 0, 8: 1} if earlier else {},
        )
        out = [vmem(flat, jnp.float32)] if part else [piece] * pieces
        total = add(f"sum_{part}", total, arrived, [done], out)
    (total,) = total
    own_energy, total, saved = call(
        functools.partial(energy_kernel, replicas),
        "energy",
        [(vmem, total)],
        [vmem((2 * shards, 1, LANES), jnp.float32), vmem(flat, jnp.float32), hbm(flat, jnp.float32)],
        microseconds=0.5,
        blocked=True,
    )
    energies = lax.all_to_all(own_energy, ("core",) + FSDP, 0, 0, tiled=True)
    total_other = lax.ppermute(total, REP, swap)
    near = groups * 2 // 3
    far = groups - near
    raw, values, turns, weights = call(
        raw_kernel,
        "raw",
        [
            (smem, rep),
            (hbm, flips),
            (hbm, saved.reshape(half_shape)),
            (hbm, total_other.reshape(half_shape)),
            (hbm, inverse),
        ],
        [
            vmem((near, rows, WIDTH), jnp.float32),
            vmem((far, rows, LANES), jnp.float32),
            vmem((far, LANES, LANES), jnp.float32),
            vmem(inverse.shape, BF),
        ],
        turned
        + [
            vmem((near, LANES, LANES), jnp.float32),
            vmem(half_shape, jnp.float32),
            vmem(half_shape, jnp.float32),
            dma((5,)),
        ],
        5.0,
    )
    update = call(
        functools.partial(update_kernel, rows * width * shards, replicas),
        "update",
        [(vmem, raw), (vmem, values), (vmem, turns), (vmem, weights), (vmem, energies)],
        hbm((rows, width), BF),
        turned + [vmem((groups, rows, WIDTH), BF), dma((groups,))],
        2.0,
    )
    return new_moment, update


def solution(mesh):
    cores = 2
    chips = mesh.shape["rep"] // cores
    lines = 4
    split = Mesh(
        mesh.devices.reshape(chips, cores, mesh.shape["fsdp"] // lines, lines), REP + FSDP
    )
    placed = (P(REP, FSDP, None), P(FSDP, None, None), P(None, FSDP, None))
    return jax.shard_map(
        per_device,
        mesh=split,
        in_specs=placed,
        out_specs=(P(REP, FSDP, None), P(FSDP, None)),
        check_vma=False,
    )
```
